128 devices in a mesh: tm: 16 (over y, x), sta: 8 (over z, core).
Axes of the slice: x: 4, y: 4, z: 4, core: 2. Of those that a mesh axis runs over, the one named last changes fastest.
Arguments:
- waveforms: bfloat16 [64, 8192], P('sta', 'tm'), may hold values from -220 to 220
- templates: bfloat16 [2048, 64, 512], P(None, 'sta'), may hold values from -6 to 6
- detection_flags: int32 [2048, 16], P('sta', 'tm'), may hold values from 0 to 1, as said below
- pair_events: int32 [2048, 2], P(('tm', 'sta')), may hold values from 0 to 2559, as said below
- pair_lags: int32 [2048], P(('tm', 'sta')), may hold values from -256 to 128
Outputs:
- network_stack: float32 [2048, 8192], P('sta', 'tm')
- pair_cc: float32 [2048, 128], P(('tm', 'sta'))
The draws below stay inside these ranges and needn't reach their ends.
Inputs may be any that keep to these rules, and one draw needn't show every extreme that they name: `detection_flags`: among the 256 templates of one station group, in every time block at least one and at most 32 flags are 1, and exactly 32 in some such block. There are exactly 16 * 8 * (32 + max(1, 8)) // 2 flags equal to 1 in all. `pair_events`: every entry is the number of a detection, below the count of flags that are 1; the first and the last detection are named. Among the 32 entries of the pairs of one owner device, at most 1 are detections of one time block and station group, and exactly 1 for some.
All inputs are finite; a program needn't handle non-finite values.
Results may differ from the reference program's by a relative error of at most 0.0003.
Values may be sent and summed in bfloat16 or wider, within the bound.
No kernel may reach another device: no remote copies, remote signals or barrier semaphores. Data moves between devices by JAX's collectives and lax.ppermute only.
A program may use at most 384 MiB of HBM per device.

```python
import jax
import jax.numpy as jnp
from jax import lax

BLK = 512
TLEN = 512
TEMPLATES = 2048
CAP = 32
NLAG = 128
PAIRS_DEV = 16
STATIONS = 64
NBLK = 16
SAMPLES = 8192
TPD = 256
NPAIRS = 2048


def device_counts(key):
    inner = jax.random.fold_in(key, 7)
    group_count = TEMPLATES // TPD
    units = NBLK * group_count
    half = units // 2
    lowest = max(1, CAP // 4)
    first_half = jax.random.randint(inner, (half,), lowest, CAP + 1)
    chosen = jax.random.randint(jax.random.fold_in(inner, 1), (), 0, half)
    first_half = jnp.where(jnp.arange(half) == chosen, CAP, first_half)
    second_half = CAP + lowest - first_half
    counts = jnp.concatenate([first_half, second_half]).astype(jnp.int32)
    return counts.reshape(NBLK, group_count)


def draw_detection_flags(key, part):
    counts = device_counts(key)
    key = jax.random.fold_in(key, 11)
    group_count = TEMPLATES // TPD
    scores = jax.random.randint(key, (group_count, TPD, NBLK), 0, 2 ** 20) * TPD
    scores = scores + jnp.arange(TPD, dtype=jnp.int32)[None, :, None]
    ordering = jnp.argsort(jnp.argsort(scores, axis=1, stable=True), axis=1, stable=True)
    picked = ordering < jnp.transpose(counts)[:, None, :]
    return picked.reshape(TEMPLATES, NBLK).astype(jnp.int32)


def draw_pair_events(key, part):
    counts = device_counts(key).reshape(-1).astype(jnp.int32)
    starts = (jnp.cumsum(counts) - counts).astype(jnp.int32)
    total = jnp.sum(counts).astype(jnp.int32)
    key = jax.random.fold_in(key, 13)
    source_count = NBLK * (TEMPLATES // TPD)
    owner_count = NPAIRS // PAIRS_DEV
    perm_key, pick_key = jax.random.split(key, 2)
    owner_keys = jax.random.split(perm_key, owner_count)
    orders = jax.vmap(lambda single: jax.random.permutation(single, source_count))(owner_keys)
    first_row = orders[0].astype(jnp.int32)
    position = jnp.arange(source_count, dtype=jnp.int32)
    sort_keys = jnp.where(first_row == source_count - 1, -2, jnp.where(first_row == 0, -1, position))
    first_row = first_row[jnp.argsort(sort_keys, stable=True)]
    orders = orders.at[0].set(first_row)
    slot_index = jnp.arange(2 * PAIRS_DEV, dtype=jnp.int32) % source_count
    sources = orders[:, slot_index].astype(jnp.int32)
    drawn = jax.random.randint(pick_key, (owner_count, 2 * PAIRS_DEV), 0, 2 ** 30)
    events = starts[sources] + drawn % counts[sources]
    events = events.at[0, 0].set(total - 1)
    events = events.at[0, 1].set(0)
    return events.reshape(NPAIRS, 2).astype(jnp.int32)


def draw_waveforms(key, part):
    key = jax.random.fold_in(key, 17)
    gain_key, noise_key = jax.random.split(key, 2)
    rising = 3.0 ** (jnp.arange(STATIONS, dtype=jnp.float32) / STATIONS)
    station_gain = 10.0 ** jax.random.uniform(gain_key, (STATIONS,)) * rising
    noise = jax.random.truncated_normal(noise_key, -6.0, 6.0, (STATIONS, SAMPLES))
    values = noise * station_gain[:, None]
    return values.astype(jnp.bfloat16)


def set_ends(entries, own_key, smallest, high):
    shape = entries.shape
    index_at = [jax.random.randint(jax.random.fold_in(own_key, axis), (), 0, shape[axis]) for axis in range(len(shape))]
    entries = entries.at[tuple(index_at)].set(smallest)
    longest = shape.index(max(shape))
    index_at[longest] = (index_at[longest] + 1) % shape[longest]
    return entries.at[tuple(index_at)].set(high)


def level_of(key, shape, cuts, least, high):
    def one(dim, shards_of):
        steps = jax.random.uniform(jax.random.fold_in(jax.random.fold_in(key, 6), dim), (shards_of,), jnp.float32, least / len(cuts), high / len(cuts))
        return jnp.repeat(jnp.exp(steps), shape[dim] // shards_of).reshape((-1,) + (1,) * (len(shape) - dim - 1))

    loudness = one(*cuts[0])
    for cut in cuts[1:]:
        loudness = loudness * one(*cut)
    return loudness


def centred(rng, dims, spread, limit, cuts=(), kind=jnp.bfloat16):
    result = jax.random.normal(rng, dims, jnp.float32) * spread
    if len(cuts) > 0:
        result = level_of(rng, dims, cuts, -0.22, 0.18) * result
    return jnp.clip(result, min=-limit, max=limit).astype(kind)


def setup_inputs(seed: int = 0) -> dict:
    key_list = jax.random.split(jax.random.key(seed), 6)
    return {
        "waveforms": draw_waveforms(jax.random.fold_in(key_list[5], 71), 0),
        "templates": centred(key_list[1], (TEMPLATES, STATIONS, TLEN), 1.0, 6.0, ((1, 8),)),
        "detection_flags": draw_detection_flags(jax.random.fold_in(key_list[5], 71), 0),
        "pair_events": draw_pair_events(jax.random.fold_in(key_list[5], 71), 0),
        "pair_lags": set_ends(jax.random.randint(key_list[4], (NPAIRS,), -(BLK // 2), BLK // 2 - NLAG + 1), jax.random.fold_in(key_list[4], 1), -(BLK // 2), (BLK // 2 - NLAG + 1) - 1).astype(jnp.int32),
    }


epsilon = 1e-06

def toeplitz(vector, height, breadth):
    length = vector.shape[-1]
    leading = vector.shape[:-1]
    copies = jnp.broadcast_to(vector[..., None, :], leading + (height, length))
    copies = copies.reshape(leading + (height * length,))
    widths = [(0, 0)] * len(leading) + [(0, height)]
    copies = jnp.pad(copies, widths)
    return copies.reshape(leading + (height, length + 1))[..., :breadth]

def lagged(earlier_win, later_win, lag_starts, block_len, lag_count):
    margin = block_len // 2
    padded = jnp.pad(later_win, ((0, 0), (margin, margin)))

    def cut_piece(values, anchor):
        return lax.dynamic_slice_in_dim(values, anchor, lag_count + block_len, 0)
    pieces = jax.vmap(cut_piece)(padded, (lag_starts + margin).astype(jnp.int32))
    shifted = toeplitz(pieces, lag_count, block_len)
    product = jnp.einsum('plk,pk->pl', shifted, earlier_win, precision=lax.Precision.HIGHEST)
    power_one = lax.optimization_barrier(jnp.mean(earlier_win * earlier_win, axis=1))
    power_two = lax.optimization_barrier(jnp.mean(later_win * later_win, axis=1))
    return product / jnp.sqrt(block_len * (power_one + epsilon) * (power_two + epsilon))[:, None]

def reference(waveforms, templates, detection_flags, pair_events, pair_lags):
    padded = jnp.pad(waveforms, ((0, 0), (0, BLK)))
    filters = templates.astype(jnp.float32)

    def one_block(block_index):
        segment = lax.dynamic_slice_in_dim(padded, block_index * BLK, 2 * BLK, 1)
        sliding = toeplitz(segment, BLK, TLEN).astype(jnp.float32)
        product = jnp.einsum('tsk,snk->tn', filters, sliding, precision=lax.Precision.HIGHEST)
        squares = lax.optimization_barrier(jnp.sum(segment.astype(jnp.float32) ** 2, axis=0))
        energy = lax.optimization_barrier(jnp.sum(toeplitz(squares, BLK, TLEN), axis=1))
        return product / jnp.sqrt(energy + epsilon)[None, :]
    blocks = lax.map(one_block, jnp.arange(NBLK, dtype=jnp.int32))
    network_stack = jnp.transpose(blocks, (1, 0, 2)).reshape(TEMPLATES, NBLK * BLK)
    flat_flags = jnp.transpose(detection_flags).reshape(-1).astype(jnp.int32)
    before = (jnp.cumsum(flat_flags) - flat_flags).astype(jnp.int32)
    total_slots = flat_flags.shape[0]
    targets = jnp.where(flat_flags == 1, before, total_slots).astype(jnp.int32)
    event_rows = jnp.zeros((total_slots,), jnp.int32).at[targets].set(jnp.arange(total_slots, dtype=jnp.int32), mode='drop')
    candidates = blocks.reshape(NBLK * TEMPLATES, BLK)
    first_win = candidates[event_rows[pair_events[:, 0]]]
    second_win = candidates[event_rows[pair_events[:, 1]]]
    groups = NPAIRS // PAIRS_DEV

    def one_group(members):
        return lagged(members[0], members[1], members[2], BLK, NLAG)
    pair_cc = lax.map(one_group, (first_win.reshape(groups, PAIRS_DEV, BLK), second_win.reshape(groups, PAIRS_DEV, BLK), pair_lags.reshape(groups, PAIRS_DEV)))
    return (network_stack, pair_cc.reshape(NPAIRS, NLAG))
```

```python
import jax
import jax.numpy as jnp
from jax import lax
from jax.experimental import pallas as pl
from jax.experimental.pallas import tpu as pltpu
from jax.sharding import PartitionSpec as P

BLK = 512
TLEN = 512
NLAG = 128
LANES = 128
EXTRA = 8
epsilon = 1e-06
BOTH = ("tm", "sta")
VMEM = pl.BlockSpec(memory_space=pltpu.VMEM)
SMEM = pl.BlockSpec(memory_space=pltpu.SMEM)
f32 = jnp.float32
bf16 = jnp.bfloat16


def params(**extra):
    return pltpu.CompilerParams(vmem_limit_bytes=56 << 20, **extra)


def whole(kernel, outs, flops, *operands, smem=0):
    return pl.pallas_call(
        kernel,
        out_shape=outs,
        in_specs=[SMEM] * smem + [VMEM] * (len(operands) - smem),
        out_specs=jax.tree.map(lambda _: VMEM, outs),
        compiler_params=params(),
        cost_estimate=pl.CostEstimate(flops=flops, bytes_accessed=1 << 20, transcendentals=0),
    )(*operands)


def left(values, distance):
    return pltpu.roll(values, values.shape[-1] - distance, values.ndim - 1)


def build(wave_ref, next_ref, sliding_ref, energy_ref):
    segment = jnp.concatenate([wave_ref[...], next_ref[...]], axis=1).astype(f32)
    stations, length = segment.shape
    down = lax.broadcasted_iota(jnp.int32, (LANES, LANES), 0)
    along = lax.broadcasted_iota(jnp.int32, (LANES, LANES), 1)
    flip = (down + along == LANES - 1).astype(f32).astype(bf16)
    for s in range(stations):
        row = jnp.broadcast_to(segment[s : s + 1], (LANES, length))
        moved = pltpu.roll(row, length - LANES + 1, 1, stride=1, stride_axis=0).astype(bf16)
        shifted = jnp.dot(flip, moved, preferred_element_type=f32).astype(bf16)
        for k in range(0, TLEN, LANES):
            sliding_ref[pl.ds(s * TLEN + k, LANES), :] = shifted[:, k : k + BLK]
    window = jnp.sum(segment * segment, axis=0, keepdims=True)
    window = jnp.broadcast_to(window, (EXTRA, length))
    width = 1
    while width < TLEN:
        window = window + left(window, width)
        width *= 2
    energy_ref[...] = window[:, :BLK]


def correlate(place_ref, templates_ref, sliding_ref, energy_ref, keep_ref, send_ref):
    group = keep_ref.shape[0] - EXTRA
    core = place_ref[1]
    base = place_ref[0] * 2 * group
    other = templates_ref[pl.ds(base + (1 - core) * group, group)]
    own = templates_ref[pl.ds(base + core * group, group)]
    filters = jnp.concatenate([other, own], axis=0).reshape(2 * group, -1)
    product = jnp.dot(filters, sliding_ref[...], preferred_element_type=f32)
    send_ref[:group] = product[:group]
    send_ref[group:] = energy_ref[...]
    keep_ref[:group] = product[group:]
    keep_ref[group:] = energy_ref[...]


def three(values):
    high = values.astype(bf16)
    rest = values - high.astype(f32)
    middle = rest.astype(bf16)
    low = (rest - middle.astype(f32)).astype(bf16)
    return high, middle, low


def pick(selector, parts):
    high, middle, low = [jnp.dot(selector, part, preferred_element_type=f32) for part in parts]
    return high + (middle + low)


def finish(place_ref, a_ref, b_ref, c_ref, d_ref, e_ref, flags_ref, info_ref, stack_ref, windows_ref):
    group = stack_ref.shape[0]
    total = (a_ref[...] + b_ref[...]) + (c_ref[...] + d_ref[...]) + e_ref[...]
    stack = total[:group] / jnp.sqrt(total[group : group + 1] + epsilon)
    stack_ref[...] = stack
    info = info_ref[:, 0, :]
    devices = info.shape[0]
    rows = lax.broadcasted_iota(jnp.int32, info.shape, 0)
    lanes = lax.broadcasted_iota(jnp.int32, info.shape, 1)
    counted = lanes == LANES - 1
    here = place_ref[2]
    start = jnp.sum(jnp.where(counted & (rows < here), info, 0))
    found = jnp.sum(jnp.where(counted & (rows == here), info, 0))
    mine = (info >= start) & (info < start + found) & (lanes < 32)
    rank = jnp.sum(jnp.where(mine, info - start + 1, 0), axis=1, keepdims=True) - 1
    flags = jnp.broadcast_to(flags_ref[...], (8, group)).astype(f32)
    earlier = lax.broadcasted_iota(jnp.int32, (group, group), 0) < lax.broadcasted_iota(
        jnp.int32, (group, group), 1
    )
    before = jnp.dot(flags.astype(bf16), earlier.astype(f32).astype(bf16), preferred_element_type=f32)
    before = jnp.where(flags > 0.5, before, -2.0)
    selector = jnp.broadcast_to(before[:1], (devices, group)) == rank.astype(f32)
    windows = pick(selector.astype(f32).astype(bf16), three(stack))
    windows_ref[:, 0, :] = windows


def cross(lags_ref, events_ref, info_ref, received_ref, out_ref):
    info = info_ref[:, 0, :]
    devices = info.shape[0]
    pairs = out_ref.shape[0]
    rows = lax.broadcasted_iota(jnp.int32, (devices, devices), 0)
    columns = lax.broadcasted_iota(jnp.int32, (devices, devices), 1)
    counts = jnp.broadcast_to(info[:, LANES - 1 :], (devices, devices))
    starts = jnp.sum(jnp.where(rows < columns, counts, 0), axis=0, keepdims=True)
    ends = jnp.sum(jnp.where(rows <= columns, counts, 0), axis=0, keepdims=True)
    events = events_ref[...]
    both = jnp.concatenate([events[:, 0:1], events[:, 1:2]], axis=0)
    selector = (starts <= both) & (both < ends)
    picked = pick(selector.astype(f32).astype(bf16), three(received_ref[:, 0, :]))
    first, second = picked[:pairs], picked[pairs:]
    lane = lax.broadcasted_iota(jnp.int32, (NLAG, LANES), 1)
    raw = jnp.zeros((NLAG, LANES), f32)
    length = 2 * BLK
    for p in range(pairs):
        row = jnp.concatenate([first[p : p + 1], jnp.zeros((1, BLK), f32)], axis=1)
        shift = lax.rem(lags_ref[p] + length, length)
        row = pltpu.roll(jnp.broadcast_to(row, (8, length)), shift, 1)
        row = jnp.broadcast_to(row[:1], (NLAG, length))
        moved = pltpu.roll(row, 0, 1, stride=1, stride_axis=0)
        sums = jnp.sum(moved[:, :BLK] * second[p : p + 1], axis=1, keepdims=True)
        raw = jnp.where(lane == p, sums, raw)
    raw = jnp.transpose(raw)[:pairs]
    power_one = jnp.mean(first * first, axis=1, keepdims=True)
    power_two = jnp.mean(second * second, axis=1, keepdims=True)
    out_ref[...] = raw / jnp.sqrt(BLK * (power_one + epsilon) * (power_two + epsilon))


def shards(waveforms, templates, detection_flags, pair_events, pair_lags):
    across = lax.axis_size("sta")
    ahead = lax.axis_size("tm")
    devices = across * ahead
    group = detection_flags.shape[0]
    station_group = lax.axis_index("sta")
    place = lax.axis_index("tm") * across + station_group
    plane, core = station_group // 2, station_group % 2
    planes = across // 2

    following = lax.ppermute(waveforms, "tm", [(i, i - 1) for i in range(1, ahead)])
    sliding, energy = whole(
        build,
        (
            jax.ShapeDtypeStruct((waveforms.shape[0] * TLEN, BLK), bf16),
            jax.ShapeDtypeStruct((EXTRA, BLK), f32),
        ),
        1 << 24,
        waveforms,
        following,
    )

    def partial(distance):
        where = jnp.stack([(plane + distance) % planes, core]).astype(jnp.int32)
        shape = jax.ShapeDtypeStruct((group + EXTRA, BLK), f32)
        keep, send = whole(
            correlate,
            (shape, shape),
            2 * 2 * group * templates.shape[1] * TLEN * BLK,
            where,
            templates,
            sliding,
            energy,
            smem=1,
        )
        return keep, lax.ppermute(send, "sta", [(i, i ^ 1) for i in range(across)])

    arrived = []
    for distance in (2, 1, 3):
        keep, came = partial(distance)
        route = [(i, (i + 2 * distance) % across) for i in range(across)]
        arrived.append(lax.ppermute(keep + came, "sta", route))
    keep, came = partial(0)

    count = jnp.sum(detection_flags)
    note = jnp.concatenate(
        [
            pair_events.reshape(-1),
            jnp.zeros((LANES - 1 - pair_events.size,), jnp.int32),
            count[None],
        ]
    )
    note = jnp.broadcast_to(note[None, None], (devices, 1, LANES))
    note, keep = lax.optimization_barrier((note, keep))
    info = lax.all_to_all(note, BOTH, 0, 0, tiled=True)

    here = jnp.stack([plane, core, place]).astype(jnp.int32)
    network_stack, windows = whole(
        finish,
        (
            jax.ShapeDtypeStruct((group, BLK), f32),
            jax.ShapeDtypeStruct((devices, 1, BLK), f32),
        ),
        1 << 24,
        here,
        keep,
        came,
        *arrived,
        detection_flags.reshape(1, group),
        info,
        smem=1,
    )
    received = lax.all_to_all(windows, BOTH, 0, 0, tiled=True)
    pair_cc = whole(
        cross,
        jax.ShapeDtypeStruct((pair_events.shape[0], NLAG), f32),
        1 << 24,
        pair_lags,
        pair_events,
        info,
        received,
        smem=1,
    )
    return (network_stack, pair_cc)


def solution(mesh):
    return jax.shard_map(
        shards,
        mesh=mesh,
        in_specs=(
            P("sta", "tm"),
            P(None, "sta", None),
            P("sta", "tm"),
            P(("tm", "sta"), None),
            P(("tm", "sta")),
        ),
        out_specs=(P("sta", "tm"), P(("tm", "sta"), None)),
        check_vma=False,
    )
```

```python
import jax
import jax.numpy as jnp
from jax import lax
from jax.experimental import pallas as pl
from jax.experimental.pallas import tpu as pltpu
from jax.sharding import PartitionSpec as P

BLK = 512
TLEN = 512
NLAG = 128
LANES = 128
EXTRA = 8
epsilon = 1e-06
BOTH = ("tm", "sta")
VMEM = pl.BlockSpec(memory_space=pltpu.VMEM)
SMEM = pl.BlockSpec(memory_space=pltpu.SMEM)
f32 = jnp.float32
bf16 = jnp.bfloat16


def whole(kernel, outs, flops, *operands, smem=0):
    return pl.pallas_call(
        kernel,
        out_shape=outs,
        in_specs=[SMEM] * smem + [VMEM] * (len(operands) - smem),
        out_specs=jax.tree.map(lambda _: VMEM, outs),
        compiler_params=pltpu.CompilerParams(vmem_limit_bytes=20 << 20),
        cost_estimate=pl.CostEstimate(flops=flops, bytes_accessed=1 << 20, transcendentals=0),
    )(*operands)


def fetch(templates_ref, held_ref, arrival):
    copy = pltpu.make_async_copy(templates_ref, held_ref, arrival)
    copy.start()
    copy.wait()


def left(values, distance):
    return pltpu.roll(values, values.shape[-1] - distance, values.ndim - 1)


def build(wave_ref, next_ref, sliding_ref, energy_ref):
    segment = jnp.concatenate([wave_ref[...], next_ref[...]], axis=1).astype(f32)
    stations, length = segment.shape
    down = lax.broadcasted_iota(jnp.int32, (LANES, LANES), 0)
    along = lax.broadcasted_iota(jnp.int32, (LANES, LANES), 1)
    flip = (down + along == LANES - 1).astype(f32).astype(bf16)
    for s in range(stations):
        row = jnp.broadcast_to(segment[s : s + 1], (LANES, length))
        moved = pltpu.roll(row, length - LANES + 1, 1, stride=1, stride_axis=0).astype(bf16)
        shifted = jnp.dot(flip, moved, preferred_element_type=f32).astype(bf16)
        for k in range(0, TLEN, LANES):
            sliding_ref[pl.ds(s * TLEN + k, LANES), :] = shifted[:, k : k + BLK]
    window = jnp.sum(segment * segment, axis=0, keepdims=True)
    window = jnp.broadcast_to(window, (EXTRA, length))
    width = 1
    while width < TLEN:
        window = window + left(window, width)
        width *= 2
    energy_ref[...] = window[:, :BLK]


def correlate(place_ref, templates_ref, sliding_ref, energy_ref, keep_ref, send_ref):
    group = keep_ref.shape[0] - EXTRA
    core = place_ref[1]
    base = place_ref[0] * 2 * group
    other = templates_ref[pl.ds(base + (1 - core) * group, group)]
    own = templates_ref[pl.ds(base + core * group, group)]
    filters = jnp.concatenate([other, own], axis=0).reshape(2 * group, -1)
    product = jnp.dot(filters, sliding_ref[...], preferred_element_type=f32)
    send_ref[:group] = product[:group]
    send_ref[group:] = energy_ref[...]
    keep_ref[:group] = product[group:]
    keep_ref[group:] = energy_ref[...]


def three(values):
    high = values.astype(bf16)
    rest = values - high.astype(f32)
    middle = rest.astype(bf16)
    low = (rest - middle.astype(f32)).astype(bf16)
    return high, middle, low


def pick(selector, parts):
    high, middle, low = [jnp.dot(selector, part, preferred_element_type=f32) for part in parts]
    return high + (middle + low)


def finish(place_ref, a_ref, b_ref, c_ref, d_ref, e_ref, flags_ref, info_ref, stack_ref, windows_ref):
    group = stack_ref.shape[0]
    total = (a_ref[...] + b_ref[...]) + (c_ref[...] + d_ref[...]) + e_ref[...]
    stack = total[:group] / jnp.sqrt(total[group : group + 1] + epsilon)
    stack_ref[...] = stack
    info = info_ref[:, 0, :]
    devices = info.shape[0]
    rows = lax.broadcasted_iota(jnp.int32, info.shape, 0)
    lanes = lax.broadcasted_iota(jnp.int32, info.shape, 1)
    counted = lanes == LANES - 1
    here = place_ref[2]
    start = jnp.sum(jnp.where(counted & (rows < here), info, 0))
    found = jnp.sum(jnp.where(counted & (rows == here), info, 0))
    mine = (info >= start) & (info < start + found) & (lanes < 32)
    rank = jnp.sum(jnp.where(mine, info - start + 1, 0), axis=1, keepdims=True) - 1
    flags = jnp.broadcast_to(flags_ref[...], (8, group)).astype(f32)
    earlier = lax.broadcasted_iota(jnp.int32, (group, group), 0) < lax.broadcasted_iota(
        jnp.int32, (group, group), 1
    )
    before = jnp.dot(flags.astype(bf16), earlier.astype(f32).astype(bf16), preferred_element_type=f32)
    before = jnp.where(flags > 0.5, before, -2.0)
    selector = jnp.broadcast_to(before[:1], (devices, group)) == rank.astype(f32)
    windows = pick(selector.astype(f32).astype(bf16), three(stack))
    windows_ref[:, 0, :] = windows


def cross(lags_ref, events_ref, info_ref, received_ref, out_ref):
    info = info_ref[:, 0, :]
    devices = info.shape[0]
    pairs = out_ref.shape[0]
    rows = lax.broadcasted_iota(jnp.int32, (devices, devices), 0)
    columns = lax.broadcasted_iota(jnp.int32, (devices, devices), 1)
    counts = jnp.broadcast_to(info[:, LANES - 1 :], (devices, devices))
    starts = jnp.sum(jnp.where(rows < columns, counts, 0), axis=0, keepdims=True)
    ends = jnp.sum(jnp.where(rows <= columns, counts, 0), axis=0, keepdims=True)
    events = events_ref[...]
    both = jnp.concatenate([events[:, 0:1], events[:, 1:2]], axis=0)
    selector = (starts <= both) & (both < ends)
    picked = pick(selector.astype(f32).astype(bf16), three(received_ref[:, 0, :]))
    first, second = picked[:pairs], picked[pairs:]
    lane = lax.broadcasted_iota(jnp.int32, (NLAG, LANES), 1)
    raw = jnp.zeros((NLAG, LANES), f32)
    length = 2 * BLK
    for p in range(pairs):
        row = jnp.concatenate([first[p : p + 1], jnp.zeros((1, BLK), f32)], axis=1)
        shift = lax.rem(lags_ref[p] + length, length)
        row = pltpu.roll(jnp.broadcast_to(row, (8, length)), shift, 1)
        row = jnp.broadcast_to(row[:1], (NLAG, length))
        moved = pltpu.roll(row, 0, 1, stride=1, stride_axis=0)
        sums = jnp.sum(moved[:, :BLK] * second[p : p + 1], axis=1, keepdims=True)
        raw = jnp.where(lane == p, sums, raw)
    raw = jnp.transpose(raw)[:pairs]
    power_one = jnp.mean(first * first, axis=1, keepdims=True)
    power_two = jnp.mean(second * second, axis=1, keepdims=True)
    out_ref[...] = raw / jnp.sqrt(BLK * (power_one + epsilon) * (power_two + epsilon))


def shards(waveforms, templates, detection_flags, pair_events, pair_lags):
    across = lax.axis_size("sta")
    ahead = lax.axis_size("tm")
    devices = across * ahead
    group = detection_flags.shape[0]
    station_group = lax.axis_index("sta")
    place = lax.axis_index("tm") * across + station_group
    plane, core = station_group // 2, station_group % 2
    planes = across // 2

    held = pl.pallas_call(
        fetch,
        out_shape=pltpu.VMEM(templates.shape, templates.dtype),
        in_specs=[pl.BlockSpec(memory_space=pltpu.HBM)],
        out_specs=VMEM,
        scratch_shapes=[pltpu.SemaphoreType.DMA],
        compiler_params=pltpu.CompilerParams(vmem_limit_bytes=20 << 20),
        cost_estimate=pl.CostEstimate(flops=0, bytes_accessed=2 * templates.size * 2, transcendentals=0),
    )(templates)
    following = lax.ppermute(waveforms, "tm", [(i, i - 1) for i in range(1, ahead)])
    sliding, energy = whole(
        build,
        (
            pltpu.VMEM((waveforms.shape[0] * TLEN, BLK), bf16),
            pltpu.VMEM((EXTRA, BLK), f32),
        ),
        1 << 24,
        waveforms,
        following,
    )

    def partial(distance, after):
        where = jnp.stack([(plane + distance) % planes, core]).astype(jnp.int32)
        where, after = lax.optimization_barrier((where, after))
        shape = pltpu.VMEM((group + EXTRA, BLK), f32)
        keep, send = whole(
            correlate,
            (shape, shape),
            2 * 2 * group * templates.shape[1] * TLEN * BLK,
            where,
            held,
            sliding,
            energy,
            smem=1,
        )
        return keep, lax.ppermute(send, "sta", [(i, i ^ 1) for i in range(across)])

    arrived = []
    order = (2, 1, 3, 0)
    keep, came = partial(order[0], ())
    for distance, following in zip(order, order[1:]):
        after = () if distance == order[0] else (total,)
        new = partial(following, after)
        total = keep + came
        route = [(i, (i + 2 * distance) % across) for i in range(across)]
        arrived.append(lax.ppermute(total, "sta", route))
        keep, came = new

    count = jnp.sum(detection_flags)
    note = jnp.concatenate(
        [
            pair_events.reshape(-1),
            jnp.zeros((LANES - 1 - pair_events.size,), jnp.int32),
            count[None],
        ]
    )
    note = jnp.broadcast_to(note[None, None], (devices, 1, LANES))
    note, _ = lax.optimization_barrier((note, total))
    info = lax.all_to_all(note, BOTH, 0, 0, tiled=True)

    here = jnp.stack([plane, core, place]).astype(jnp.int32)
    network_stack, windows = whole(
        finish,
        (
            jax.ShapeDtypeStruct((group, BLK), f32),
            jax.ShapeDtypeStruct((devices, 1, BLK), f32),
        ),
        1 << 24,
        here,
        keep,
        came,
        *arrived,
        detection_flags.reshape(1, group),
        info,
        smem=1,
    )
    received = lax.all_to_all(windows, BOTH, 0, 0, tiled=True)
    pair_cc = whole(
        cross,
        jax.ShapeDtypeStruct((pair_events.shape[0], NLAG), f32),
        1 << 24,
        pair_lags,
        pair_events,
        info,
        received,
        smem=1,
    )
    return (network_stack, pair_cc)


def solution(mesh):
    return jax.shard_map(
        shards,
        mesh=mesh,
        in_specs=(
            P("sta", "tm"),
            P(None, "sta", None),
            P("sta", "tm"),
            P(("tm", "sta"), None),
            P(("tm", "sta")),
        ),
        out_specs=(P("sta", "tm"), P(("tm", "sta"), None)),
        check_vma=False,
    )
```

```python
import functools

import jax
import jax.numpy as jnp
from jax import lax
from jax.experimental import pallas as pl
from jax.experimental.pallas import tpu as pltpu
from jax.sharding import PartitionSpec as P

BLK = 512
TLEN = 512
NLAG = 128
LANES = 128
EXTRA = 8
epsilon = 1e-06
BOTH = ("tm", "sta")
VMEM = pl.BlockSpec(memory_space=pltpu.VMEM)
SMEM = pl.BlockSpec(memory_space=pltpu.SMEM)
f32 = jnp.float32
bf16 = jnp.bfloat16


def whole(kernel, outs, flops, *operands, smem=0, scratch=()):
    return pl.pallas_call(
        kernel,
        out_shape=outs,
        in_specs=[SMEM] * smem + [VMEM] * (len(operands) - smem),
        out_specs=jax.tree.map(lambda _: VMEM, outs),
        scratch_shapes=scratch,
        compiler_params=pltpu.CompilerParams(vmem_limit_bytes=20 << 20),
        cost_estimate=pl.CostEstimate(flops=flops, bytes_accessed=1 << 20, transcendentals=0),
    )(*operands)


def left(values, distance):
    return pltpu.roll(values, values.shape[-1] - distance, values.ndim - 1)


def build(segment, sliding_ref):
    stations, length = segment.shape
    down = lax.broadcasted_iota(jnp.int32, (LANES, LANES), 0)
    along = lax.broadcasted_iota(jnp.int32, (LANES, LANES), 1)
    flip = (down + along == LANES - 1).astype(f32).astype(bf16)
    for s in range(stations):
        row = jnp.broadcast_to(segment[s : s + 1], (LANES, length))
        moved = pltpu.roll(row, length - LANES + 1, 1, stride=1, stride_axis=0).astype(bf16)
        shifted = jnp.dot(flip, moved, preferred_element_type=f32).astype(bf16)
        for k in range(0, TLEN, LANES):
            sliding_ref[pl.ds(s * TLEN + k, LANES), :] = shifted[:, k : k + BLK]


def energy_of(segment):
    window = jnp.sum(segment * segment, axis=0, keepdims=True)
    window = jnp.broadcast_to(window, (EXTRA, window.shape[1]))
    width = 1
    while width < TLEN:
        window = window + left(window, width)
        width *= 2
    return window[:, :BLK]


def correlate(distances, here_ref, wave_ref, next_ref, templates_ref, *rest):
    planes = len(distances)
    if len(rest) > 5:
        flags_ref, events_ref, keep_ref, send_ref, note_ref, held, sliding, arrival = rest
    else:
        keep_ref, send_ref, held, sliding, arrival = rest
    group = keep_ref.shape[1] - EXTRA
    plane, core, around = here_ref[0], here_ref[1], here_ref[3]

    def copy(i, half):
        chip = lax.rem(plane + distances[i], around)
        first = (chip * 2 + (1 - core if half == 0 else core)) * group
        return pltpu.make_async_copy(
            templates_ref.at[pl.ds(first, group)], held.at[i, half], arrival.at[i, half]
        )

    for i in range(planes):
        for half in range(2):
            copy(i, half).start()
    segment = jnp.concatenate([wave_ref[...], next_ref[...]], axis=1).astype(f32)
    build(segment, sliding)
    energy = energy_of(segment)
    if len(rest) > 5:
        fill = jnp.zeros((2, LANES - events_ref.shape[1]), jnp.int32)
        events = jnp.concatenate([events_ref[...], fill], axis=1)
        count = jnp.sum(flags_ref[...], axis=1, keepdims=True)
        lane = lax.broadcasted_iota(jnp.int32, (1, LANES), 1)
        note = events[0:1] + pltpu.roll(events, events_ref.shape[1], 1)[1:2]
        note = jnp.where(lane == LANES - 1, count, note)
        note_ref[...] = jnp.broadcast_to(note[None], note_ref.shape)
    for i in range(planes):
        for half, out_ref in enumerate((send_ref, keep_ref)):
            copy(i, half).wait()
            filters = held[i, half].reshape(group, -1)
            out_ref[i, :group] = jnp.dot(filters, sliding[...], preferred_element_type=f32)
            out_ref[i, group:] = energy


def merge(keep_ref, came_ref, *sum_refs):
    for i, sum_ref in enumerate(sum_refs):
        sum_ref[...] = keep_ref[i] + came_ref[i]


def three(values):
    high = values.astype(bf16)
    rest = values - high.astype(f32)
    middle = rest.astype(bf16)
    low = (rest - middle.astype(f32)).astype(bf16)
    return high, middle, low


def pick(selector, parts):
    high, middle, low = [jnp.dot(selector, part, preferred_element_type=f32) for part in parts]
    return high + (middle + low)


def finish(place_ref, a_ref, b_ref, c_ref, d_ref, e_ref, flags_ref, info_ref, stack_ref, windows_ref):
    group = stack_ref.shape[0]
    total = (a_ref[...] + b_ref[...]) + (c_ref[...] + d_ref[...]) + e_ref[...]
    stack = total[:group] / jnp.sqrt(total[group : group + 1] + epsilon)
    stack_ref[...] = stack
    info = info_ref[:, 0, :]
    devices = info.shape[0]
    rows = lax.broadcasted_iota(jnp.int32, info.shape, 0)
    lanes = lax.broadcasted_iota(jnp.int32, info.shape, 1)
    counted = lanes == LANES - 1
    here = place_ref[2]
    start = jnp.sum(jnp.where(counted & (rows < here), info, 0))
    found = jnp.sum(jnp.where(counted & (rows == here), info, 0))
    mine = (info >= start) & (info < start + found) & (lanes < 32)
    rank = jnp.sum(jnp.where(mine, info - start + 1, 0), axis=1, keepdims=True) - 1
    flags = jnp.broadcast_to(flags_ref[...], (8, group)).astype(f32)
    earlier = lax.broadcasted_iota(jnp.int32, (group, group), 0) < lax.broadcasted_iota(
        jnp.int32, (group, group), 1
    )
    before = jnp.dot(flags.astype(bf16), earlier.astype(f32).astype(bf16), preferred_element_type=f32)
    before = jnp.where(flags > 0.5, before, -2.0)
    selector = jnp.broadcast_to(before[:1], (devices, group)) == rank.astype(f32)
    windows = pick(selector.astype(f32).astype(bf16), three(stack))
    windows_ref[:, 0, :] = windows


def cross(lags_ref, events_ref, info_ref, received_ref, out_ref, turned, products):
    info = info_ref[:, 0, :]
    devices = info.shape[0]
    pairs = out_ref.shape[0]
    rows = lax.broadcasted_iota(jnp.int32, (devices, devices), 0)
    columns = lax.broadcasted_iota(jnp.int32, (devices, devices), 1)
    counts = jnp.broadcast_to(info[:, LANES - 1 :], (devices, devices))
    starts = jnp.sum(jnp.where(rows < columns, counts, 0), axis=0, keepdims=True)
    ends = jnp.sum(jnp.where(rows <= columns, counts, 0), axis=0, keepdims=True)
    square = lax.broadcasted_iota(jnp.int32, (pairs, pairs), 0) == lax.broadcasted_iota(
        jnp.int32, (pairs, pairs), 1
    )
    both = jnp.concatenate(
        [
            jnp.sum(jnp.where(square, events_ref[i : i + 1], 0), axis=1, keepdims=True)
            for i in range(2)
        ],
        axis=0,
    )
    selector = (starts <= both) & (both < ends)
    picked = pick(selector.astype(f32).astype(bf16), three(received_ref[:, 0, :]))
    first, second = picked[:pairs], picked[pairs:]
    length = 2 * BLK
    nothing = jnp.zeros((pairs, BLK), f32)
    ahead = jnp.concatenate([first, nothing], axis=1)
    behind = jnp.concatenate([second, nothing], axis=1)

    def near(values):
        return jnp.concatenate([values[:, length - NLAG :], values[:, :BLK]], axis=1)

    for u in range(NLAG // 8):
        turned[u] = near(behind if u == 0 else left(behind, 8 * u))
    for p in range(pairs):
        shift = lax.rem(lags_ref[p] + length, length)
        moved = pltpu.roll(jnp.broadcast_to(ahead[p : p + 1], (8, length)), shift, 1)
        moved = near(pltpu.roll(moved, 0, 1, stride=1, stride_axis=0))
        for u in range(NLAG // 8):
            product = moved * turned[u, pl.ds(p, 1), :]
            part = product[:, :LANES]
            for k in range(LANES, NLAG + BLK, LANES):
                part = part + product[:, k : k + LANES]
            products[pl.ds(p * NLAG + 8 * u, 8), :] = part
    ones = jnp.ones((8, LANES), bf16)
    high, middle, low = [
        lax.dot_general(ones, part, (((1,), (1,)), ((), ())), preferred_element_type=f32)
        for part in three(products[...])
    ]
    raw = high + (middle + low)
    raw = jnp.concatenate([raw[:1, p * NLAG : (p + 1) * NLAG] for p in range(pairs)], axis=0)
    power_one = jnp.mean(first * first, axis=1, keepdims=True)
    power_two = jnp.mean(second * second, axis=1, keepdims=True)
    out_ref[...] = raw / jnp.sqrt(BLK * (power_one + epsilon) * (power_two + epsilon))


def shards(waveforms, templates, detection_flags, pair_events, pair_lags):
    across = lax.axis_size("sta")
    ahead = lax.axis_size("tm")
    devices = across * ahead
    group = detection_flags.shape[0]
    station_group = lax.axis_index("sta")
    place = lax.axis_index("tm") * across + station_group
    plane, core = station_group // 2, station_group % 2
    planes = across // 2

    following = lax.ppermute(waveforms, "tm", [(i, i - 1) for i in range(1, ahead)])

    here = jnp.stack([plane, core, place, planes]).astype(jnp.int32)
    flags = detection_flags.reshape(1, group)
    events = pair_events.T

    def partial(distances, here, *others):
        count = len(distances)
        shape = jax.ShapeDtypeStruct((count, group + EXTRA, BLK), f32)
        stations = templates.shape[1]
        note = (jax.ShapeDtypeStruct((devices, 1, LANES), jnp.int32),) if others else ()
        return pl.pallas_call(
            functools.partial(correlate, distances),
            out_shape=(shape, shape) + note,
            in_specs=[SMEM, VMEM, VMEM, pl.BlockSpec(memory_space=pltpu.HBM)] + [VMEM] * len(others),
            out_specs=(VMEM, VMEM) + (VMEM,) * len(note),
            scratch_shapes=[
                pltpu.VMEM((count, 2, group, stations, TLEN), bf16),
                pltpu.VMEM((stations * TLEN, BLK), bf16),
                pltpu.SemaphoreType.DMA((count, 2)),
            ],
            compiler_params=pltpu.CompilerParams(vmem_limit_bytes=52 << 20),
            cost_estimate=pl.CostEstimate(
                flops=count * 4 * group * stations * TLEN * BLK,
                bytes_accessed=count * 4 * group * stations * TLEN,
                transcendentals=0,
            ),
        )(here, waveforms, following, templates, *others)

    def over(distance, values):
        return lax.ppermute(values, "sta", [(i, (i + 2 * distance) % across) for i in range(across)])

    def swap(values):
        return lax.ppermute(values, "sta", [(i, i ^ 1) for i in range(across)])

    away = (2, 1, 3)
    keeps, sends, note = partial(away, here, flags, events)
    cames = swap(sends)
    later, _ = lax.optimization_barrier((here, keeps))
    keep, send = partial((0,), later)
    came = swap(send)
    shape = jax.ShapeDtypeStruct(keep.shape[1:], f32)
    cames, _ = lax.optimization_barrier((cames, keep))
    sums = whole(merge, (shape,) * len(away), 1 << 20, keeps, cames)
    arrived = [over(distance, values) for distance, values in zip(away, sums)]

    note, _ = lax.optimization_barrier((note, sums))
    info = lax.all_to_all(note, BOTH, 0, 0, tiled=True)

    network_stack, windows = whole(
        finish,
        (
            jax.ShapeDtypeStruct((group, BLK), f32),
            jax.ShapeDtypeStruct((devices, 1, BLK), f32),
        ),
        1 << 24,
        here,
        keep[0],
        came[0],
        *arrived,
        flags,
        info,
        smem=1,
    )
    received = lax.all_to_all(windows, BOTH, 0, 0, tiled=True)
    pairs = pair_events.shape[0]
    pair_cc = whole(
        cross,
        jax.ShapeDtypeStruct((pairs, NLAG), f32),
        1 << 24,
        pair_lags,
        events,
        info,
        received,
        smem=1,
        scratch=[
            pltpu.VMEM((NLAG // 8, pairs, NLAG + BLK), f32),
            pltpu.VMEM((pairs * NLAG, LANES), f32),
        ],
    )
    return (network_stack, pair_cc)


def solution(mesh):
    return jax.shard_map(
        shards,
        mesh=mesh,
        in_specs=(
            P("sta", "tm"),
            P(None, "sta", None),
            P("sta", "tm"),
            P(("tm", "sta"), None),
            P(("tm", "sta")),
        ),
        out_specs=(P("sta", "tm"), P(("tm", "sta"), None)),
        check_vma=False,
    )
```

```python
import functools

import jax
import jax.numpy as jnp
from jax import lax
from jax.experimental import pallas as pl
from jax.experimental.pallas import tpu as pltpu
from jax.sharding import PartitionSpec as P

BLK = 512
TLEN = 512
NLAG = 128
LANES = 128
STEPS = 32767.0
epsilon = 1e-06
BOTH = ("tm", "sta")
VMEM = pl.BlockSpec(memory_space=pltpu.VMEM)
SMEM = pl.BlockSpec(memory_space=pltpu.SMEM)
f32 = jnp.float32
bf16 = jnp.bfloat16


def whole(kernel, outs, flops, *operands, smem=0, scratch=()):
    return pl.pallas_call(
        kernel,
        out_shape=outs,
        in_specs=[SMEM] * smem + [VMEM] * (len(operands) - smem),
        out_specs=jax.tree.map(lambda _: VMEM, outs),
        scratch_shapes=scratch,
        compiler_params=pltpu.CompilerParams(vmem_limit_bytes=20 << 20),
        cost_estimate=pl.CostEstimate(flops=flops, bytes_accessed=1 << 20, transcendentals=0),
    )(*operands)


def left(values, distance):
    return pltpu.roll(values, values.shape[-1] - distance, values.ndim - 1)


def build(segment, sliding_ref):
    stations, length = segment.shape
    down = lax.broadcasted_iota(jnp.int32, (LANES, LANES), 0)
    along = lax.broadcasted_iota(jnp.int32, (LANES, LANES), 1)
    flip = (down + along == LANES - 1).astype(f32).astype(bf16)
    for s in range(stations):
        row = jnp.broadcast_to(segment[s : s + 1], (LANES, length))
        moved = pltpu.roll(row, length - LANES + 1, 1, stride=1, stride_axis=0).astype(bf16)
        shifted = jnp.dot(flip, moved, preferred_element_type=f32).astype(bf16)
        for k in range(0, TLEN, LANES):
            sliding_ref[pl.ds(s * TLEN + k, LANES), :] = shifted[:, k : k + BLK]


def announce(flags_ref, events_ref, note_ref):
    fill = jnp.zeros((2, LANES - events_ref.shape[1]), jnp.int32)
    events = jnp.concatenate([events_ref[...], fill], axis=1)
    count = jnp.sum(flags_ref[...], axis=1, keepdims=True)
    lane = lax.broadcasted_iota(jnp.int32, (1, LANES), 1)
    words = events[0:1] + pltpu.roll(events, events_ref.shape[1], 1)[1:2]
    words = jnp.where(lane == LANES - 1, count, words)
    note_ref[...] = jnp.broadcast_to(words[None], note_ref.shape)


def sums_of_window(squares):
    window = jnp.broadcast_to(squares, (8, squares.shape[1]))
    width = 1
    while width < TLEN:
        window = window + left(window, width)
        width *= 2
    return window[:, :BLK]


def correlate(distances, here_ref, wave_ref, next_ref, templates_ref, keep_ref, send_ref, waves, held, sliding, arrival):
    planes = len(distances)
    group = held.shape[2]
    plane, core, around = here_ref[0], here_ref[1], here_ref[3]

    def copy(i, half):
        chip = lax.rem(plane + distances[i], around)
        first = (chip * 2 + (1 - core if half == 0 else core)) * group
        return pltpu.make_async_copy(
            templates_ref.at[pl.ds(first, group)], held.at[i, half], arrival.at[i, half]
        )

    pieces = [
        pltpu.make_async_copy(wave_ref, waves.at[0], arrival.at[planes, 0]),
        pltpu.make_async_copy(next_ref, waves.at[1], arrival.at[planes, 1]),
    ]
    for piece in pieces:
        piece.start()
    for i in range(planes):
        for half in range(2):
            copy(i, half).start()
    for piece in pieces:
        piece.wait()
    segment = jnp.concatenate([waves[0], waves[1]], axis=1).astype(f32)
    build(segment, sliding)
    if keep_ref.shape[0] > planes * group:
        energy = sums_of_window(jnp.sum(segment * segment, axis=0, keepdims=True))
        keep_ref[planes * group :] = energy
        send_ref[planes * group :] = energy
    for i in range(planes):
        for half, out_ref in enumerate((send_ref, keep_ref)):
            copy(i, half).wait()
            filters = held[i, half].reshape(group, -1)
            out_ref[i * group : (i + 1) * group] = jnp.dot(
                filters, sliding[...], preferred_element_type=f32
            )


def diagonal(size):
    rows = lax.broadcasted_iota(jnp.int32, (size, size), 0)
    return rows == lax.broadcasted_iota(jnp.int32, (size, size), 1)


def merge(keep_ref, came_ref, energy_ref, *code_refs):
    half = code_refs[0].shape[0] - 8
    group = 2 * half
    square = diagonal(group)
    last = len(code_refs) * group
    energy = keep_ref[last:] + came_ref[last:]
    energy_ref[...] = energy
    logarithm = jnp.log2(jnp.maximum(energy, 1e-30))
    sample = jnp.round(4.0 * logarithm)
    level = jnp.exp2(sample[:1] * -0.125)
    power = jnp.floor(logarithm)
    bits = jnp.round(energy * jnp.exp2(23.0 - power))
    row = lax.broadcasted_iota(jnp.int32, (8, BLK), 0)
    below = jnp.where(row == 1, sample, jnp.where(row == 2, power, bits)).astype(jnp.int32)
    for i, code_ref in enumerate(code_refs):
        here = slice(i * group, (i + 1) * group)
        values = (keep_ref[here] + came_ref[here]) * level
        largest = jnp.max(jnp.abs(values), axis=1, keepdims=True)
        exponent = jnp.floor(8.0 * jnp.log2(jnp.maximum(largest, 1e-30)) + 0.01) + 1.0
        codes = jnp.round(values * (STEPS * jnp.exp2(exponent * -0.125))).astype(jnp.int32)
        code_ref[:half] = (codes[:half] & 0xFFFF) | lax.shift_left(codes[half:], 16)
        exponents = jnp.sum(jnp.where(square, exponent, 0.0), axis=0, keepdims=True)
        exponents = jnp.broadcast_to(exponents.astype(jnp.int32), (8, group))
        exponents = jnp.concatenate([exponents] * (BLK // group), axis=1)
        code_ref[half:] = jnp.where(row == 0, exponents, below)


def decode(code_ref, square):
    half = code_ref.shape[0] - 8
    words = code_ref[:half]
    codes = jnp.concatenate(
        [lax.shift_right_arithmetic(lax.shift_left(words, 16), 16), lax.shift_right_arithmetic(words, 16)],
        axis=0,
    )
    below = code_ref[half:].astype(f32)
    exponent = jnp.sum(jnp.where(square, below[:1, : 2 * half], 0.0), axis=1, keepdims=True)
    level = jnp.exp2(below[1:2] * 0.125)
    energy = below[3:4] * jnp.exp2(below[2:3] - 23.0)
    return codes.astype(f32) * (jnp.exp2(exponent * 0.125) * (1.0 / STEPS)) * level, energy


def three(values):
    high = values.astype(bf16)
    rest = values - high.astype(f32)
    middle = rest.astype(bf16)
    low = (rest - middle.astype(f32)).astype(bf16)
    return high, middle, low


def pick(selector, parts):
    high, middle, low = [jnp.dot(selector, part, preferred_element_type=f32) for part in parts]
    return high + (middle + low)


def finish(here_ref, keep_ref, came_ref, energy_ref, a_ref, b_ref, c_ref, flags_ref, info_ref, stack_ref, windows_ref):
    group = stack_ref.shape[0]
    square = diagonal(group)
    stack = keep_ref[...] + came_ref[...]
    energy = energy_ref[:1]
    for code_ref in (a_ref, b_ref, c_ref):
        values, more = decode(code_ref, square)
        stack = stack + values
        energy = energy + more
    stack = stack * (1.0 / jnp.sqrt(energy + epsilon))
    stack_ref[...] = stack
    info = info_ref[:, 0, :]
    devices = info.shape[0]
    rows = lax.broadcasted_iota(jnp.int32, info.shape, 0)
    lanes = lax.broadcasted_iota(jnp.int32, info.shape, 1)
    counted = lanes == LANES - 1
    here = here_ref[2]
    start = jnp.sum(jnp.where(counted & (rows < here), info, 0))
    found = jnp.sum(jnp.where(counted & (rows == here), info, 0))
    mine = (info >= start) & (info < start + found) & (lanes < 32)
    rank = jnp.sum(jnp.where(mine, info - start + 1, 0), axis=1, keepdims=True) - 1
    flags = jnp.broadcast_to(flags_ref[...], (8, group)).astype(f32)
    earlier = lax.broadcasted_iota(jnp.int32, (group, group), 0) < lax.broadcasted_iota(
        jnp.int32, (group, group), 1
    )
    before = jnp.dot(flags.astype(bf16), earlier.astype(f32).astype(bf16), preferred_element_type=f32)
    before = jnp.where(flags > 0.5, before, -2.0)
    selector = jnp.broadcast_to(before[:1], (devices, group)) == rank.astype(f32)
    windows = pick(selector.astype(f32).astype(bf16), three(stack))
    windows_ref[:, 0, :] = windows


def cross(lags_ref, events_ref, info_ref, received_ref, out_ref, turned, products):
    info = info_ref[:, 0, :]
    devices = info.shape[0]
    pairs = out_ref.shape[0]
    rows = lax.broadcasted_iota(jnp.int32, (devices, devices), 0)
    columns = lax.broadcasted_iota(jnp.int32, (devices, devices), 1)
    counts = jnp.broadcast_to(info[:, LANES - 1 :], (devices, devices))
    starts = jnp.sum(jnp.where(rows < columns, counts, 0), axis=0, keepdims=True)
    ends = jnp.sum(jnp.where(rows <= columns, counts, 0), axis=0, keepdims=True)
    square = diagonal(pairs)
    both = jnp.concatenate(
        [
            jnp.sum(jnp.where(square, events_ref[i : i + 1], 0), axis=1, keepdims=True)
            for i in range(2)
        ],
        axis=0,
    )
    selector = (starts <= both) & (both < ends)
    picked = pick(selector.astype(f32).astype(bf16), three(received_ref[:, 0, :]))
    first, second = picked[:pairs], picked[pairs:]
    length = 2 * BLK
    nothing = jnp.zeros((pairs, BLK), f32)
    ahead = jnp.concatenate([first, nothing], axis=1)
    behind = jnp.concatenate([second, nothing], axis=1)

    def near(values):
        return jnp.concatenate([values[:, length - NLAG :], values[:, :BLK]], axis=1)

    for u in range(NLAG // 8):
        turned[u] = near(behind if u == 0 else left(behind, 8 * u))
    for p in range(pairs):
        shift = lax.rem(lags_ref[p] + length, length)
        moved = pltpu.roll(jnp.broadcast_to(ahead[p : p + 1], (8, length)), shift, 1)
        moved = near(pltpu.roll(moved, 0, 1, stride=1, stride_axis=0))
        for u in range(NLAG // 8):
            product = moved * turned[u, pl.ds(p, 1), :]
            part = product[:, :LANES]
            for k in range(LANES, NLAG + BLK, LANES):
                part = part + product[:, k : k + LANES]
            products[pl.ds(p * NLAG + 8 * u, 8), :] = part
    ones = jnp.ones((8, LANES), bf16)
    high, middle, low = [
        lax.dot_general(ones, part, (((1,), (1,)), ((), ())), preferred_element_type=f32)
        for part in three(products[...])
    ]
    raw = high + (middle + low)
    raw = jnp.concatenate([raw[:1, p * NLAG : (p + 1) * NLAG] for p in range(pairs)], axis=0)
    power_one = jnp.mean(first * first, axis=1, keepdims=True)
    power_two = jnp.mean(second * second, axis=1, keepdims=True)
    out_ref[...] = raw / jnp.sqrt(BLK * (power_one + epsilon) * (power_two + epsilon))


def shards(waveforms, templates, detection_flags, pair_events, pair_lags):
    across = lax.axis_size("sta")
    ahead = lax.axis_size("tm")
    devices = across * ahead
    group = detection_flags.shape[0]
    station_group = lax.axis_index("sta")
    place = lax.axis_index("tm") * across + station_group
    plane, core = station_group // 2, station_group % 2
    planes = across // 2

    following = lax.ppermute(waveforms, "tm", [(i, i - 1) for i in range(1, ahead)])

    here = jnp.stack([plane, core, place, planes]).astype(jnp.int32)
    flags = detection_flags.reshape(1, group)
    events = pair_events.T

    def partial(distances, here, below):
        count = len(distances)
        shape = pltpu.VMEM((count * group + below, BLK), f32)
        stations = templates.shape[1]
        return pl.pallas_call(
            functools.partial(correlate, distances),
            out_shape=(shape, shape),
            in_specs=[SMEM] + [pl.BlockSpec(memory_space=pl.ANY)] * 2 + [pl.BlockSpec(memory_space=pltpu.HBM)],
            out_specs=(VMEM, VMEM),
            scratch_shapes=[
                pltpu.VMEM((2, stations, BLK), bf16),
                pltpu.VMEM((count, 2, group, stations, TLEN), bf16),
                pltpu.VMEM((stations * TLEN, BLK), bf16),
                pltpu.SemaphoreType.DMA((count + 1, 2)),
            ],
            compiler_params=pltpu.CompilerParams(vmem_limit_bytes=48 << 20),
            cost_estimate=pl.CostEstimate(
                flops=count * 4 * group * stations * TLEN * BLK,
                bytes_accessed=count * 4 * group * stations * TLEN,
                transcendentals=0,
            ),
        )(here, waveforms, following, templates)

    def over(distance, values):
        return lax.ppermute(values, "sta", [(i, (i + 2 * distance) % across) for i in range(across)])

    def swap(values):
        return lax.ppermute(values, "sta", [(i, i ^ 1) for i in range(across)])

    away = (2, 1, 3)
    keeps, sends = partial(away, here, 8)
    cames = swap(sends)
    later, _ = lax.optimization_barrier((here, keeps))
    keep, send = partial((0,), later, 0)
    came = swap(send)
    cames, _ = lax.optimization_barrier((cames, keep))
    shape = jax.ShapeDtypeStruct((group // 2 + 8, BLK), jnp.int32)
    energy, *codes = whole(
        merge, (jax.ShapeDtypeStruct((8, BLK), f32),) + (shape,) * len(away), 1 << 22, keeps, cames
    )
    arrived = [over(distance, values) for distance, values in zip(away, codes)]

    note = whole(announce, jax.ShapeDtypeStruct((devices, 1, LANES), jnp.int32), 1 << 20, flags, events)
    note, _ = lax.optimization_barrier((note, codes))
    info = lax.all_to_all(note, BOTH, 0, 0, tiled=True)

    network_stack, windows = whole(
        finish,
        (
            jax.ShapeDtypeStruct((group, BLK), f32),
            jax.ShapeDtypeStruct((devices, 1, BLK), f32),
        ),
        1 << 24,
        here,
        keep,
        came,
        energy,
        *arrived,
        flags,
        info,
        smem=1,
    )
    received = lax.all_to_all(windows, BOTH, 0, 0, tiled=True)
    pairs = pair_events.shape[0]
    pair_cc = whole(
        cross,
        jax.ShapeDtypeStruct((pairs, NLAG), f32),
        1 << 24,
        pair_lags,
        events,
        info,
        received,
        smem=1,
        scratch=[
            pltpu.VMEM((NLAG // 8, pairs, NLAG + BLK), f32),
            pltpu.VMEM((pairs * NLAG, LANES), f32),
        ],
    )
    return (network_stack, pair_cc)


def solution(mesh):
    return jax.shard_map(
        shards,
        mesh=mesh,
        in_specs=(
            P("sta", "tm"),
            P(None, "sta", None),
            P("sta", "tm"),
            P(("tm", "sta"), None),
            P(("tm", "sta")),
        ),
        out_specs=(P("sta", "tm"), P(("tm", "sta"), None)),
        check_vma=False,
    )
```

```python
import functools

import jax
import jax.numpy as jnp
from jax import lax
from jax.experimental import pallas as pl
from jax.experimental.pallas import tpu as pltpu
from jax.sharding import PartitionSpec as P

BLK = 512
TLEN = 512
NLAG = 128
LANES = 128
SLOT = 64
WORDS = 4
STEPS = 32767.0
epsilon = 1e-06
VMEM = pl.BlockSpec(memory_space=pltpu.VMEM)
SMEM = pl.BlockSpec(memory_space=pltpu.SMEM)
f32 = jnp.float32
bf16 = jnp.bfloat16


def whole(kernel, outs, flops, *operands, smem=0, scratch=()):
    return pl.pallas_call(
        kernel,
        out_shape=outs,
        in_specs=[SMEM] * smem + [VMEM] * (len(operands) - smem),
        out_specs=jax.tree.map(lambda _: VMEM, outs),
        scratch_shapes=scratch,
        compiler_params=pltpu.CompilerParams(vmem_limit_bytes=20 << 20),
        cost_estimate=pl.CostEstimate(flops=flops, bytes_accessed=1 << 20, transcendentals=0),
    )(*operands)


def left(values, distance):
    return pltpu.roll(values, values.shape[-1] - distance, values.ndim - 1)


def build(segment, sliding_ref):
    stations, length = segment.shape
    down = lax.broadcasted_iota(jnp.int32, (LANES, LANES), 0)
    along = lax.broadcasted_iota(jnp.int32, (LANES, LANES), 1)
    flip = (down + along == LANES - 1).astype(f32).astype(bf16)
    for s in range(stations):
        row = jnp.broadcast_to(segment[s : s + 1], (LANES, length))
        moved = pltpu.roll(row, length - LANES + 1, 1, stride=1, stride_axis=0).astype(bf16)
        shifted = jnp.dot(flip, moved, preferred_element_type=f32).astype(bf16)
        for k in range(0, TLEN, LANES):
            sliding_ref[pl.ds(s * TLEN + k, LANES), :] = shifted[:, k : k + BLK]


def announce(wave_ref, flags_ref, events_ref, words_ref, held_ref):
    held_ref[...] = wave_ref[...]
    fill = jnp.zeros((2, LANES - events_ref.shape[1]), f32)
    words = jnp.concatenate([events_ref[...].astype(f32), fill], axis=1)
    words = words[0:1] + pltpu.roll(words, events_ref.shape[1], 1)[1:2]
    count = jnp.sum(flags_ref[...].astype(f32), axis=1, keepdims=True)
    lane = lax.broadcasted_iota(jnp.int32, words.shape, 1)
    words_ref[...] = jnp.broadcast_to(jnp.where(lane == SLOT - 1, count, words), words_ref.shape)


def sums_of_window(squares):
    window = jnp.broadcast_to(squares, (8, squares.shape[1]))
    width = 1
    while width < TLEN:
        window = window + left(window, width)
        width *= 2
    return window[:, :BLK]


def correlate(distances, here_ref, wave_ref, next_ref, words_ref, templates_ref, keep_ref, send_ref, waves, held, sliding, arrival):
    planes = len(distances)
    group = held.shape[2]
    plane, core, around = here_ref[0], here_ref[1], here_ref[3]

    def copy(i, half):
        chip = lax.rem(plane + distances[i], around)
        first = (chip * 2 + (1 - core if half == 0 else core)) * group
        return pltpu.make_async_copy(
            templates_ref.at[pl.ds(first, group)], held.at[i, half], arrival.at[i, half]
        )

    pieces = [
        pltpu.make_async_copy(wave_ref, waves.at[0], arrival.at[planes, 0]),
        pltpu.make_async_copy(next_ref, waves.at[1], arrival.at[planes, 1]),
    ]
    for piece in pieces:
        piece.start()
    for i in range(planes):
        for half in range(2):
            copy(i, half).start()
    for piece in pieces:
        piece.wait()
    segment = jnp.concatenate([waves[0], waves[1]], axis=1).astype(f32)
    build(segment, sliding)
    if keep_ref.shape[0] > planes * group:
        energy = sums_of_window(jnp.sum(segment * segment, axis=0, keepdims=True))
        words = jnp.concatenate([words_ref[...]] * (BLK // LANES), axis=1)
        row = lax.broadcasted_iota(jnp.int32, energy.shape, 0)
        below = jnp.where(row == WORDS, words, energy)
        keep_ref[planes * group :] = below
        send_ref[planes * group :] = below
    for i in range(planes):
        for half, out_ref in enumerate((send_ref, keep_ref)):
            copy(i, half).wait()
            filters = held[i, half].reshape(group, -1)
            out_ref[i * group : (i + 1) * group] = jnp.dot(
                filters, sliding[...], preferred_element_type=f32
            )


def diagonal(size):
    rows = lax.broadcasted_iota(jnp.int32, (size, size), 0)
    return rows == lax.broadcasted_iota(jnp.int32, (size, size), 1)


def merge(keep_ref, came_ref, energy_ref, note_ref, *code_refs):
    half = code_refs[0].shape[0] - 8
    group = 2 * half
    square = diagonal(group)
    last = len(code_refs) * group
    energy = keep_ref[last:] + came_ref[last:]
    energy_ref[...] = energy
    words = [ref[last + WORDS : last + WORDS + 1, :LANES].astype(jnp.int32) for ref in (keep_ref, came_ref)]
    lane = lax.broadcasted_iota(jnp.int32, (1, LANES), 1)
    words = jnp.where(lane < SLOT, words[0], pltpu.roll(words[1], SLOT, 1))
    words = jnp.concatenate([words] * (note_ref.shape[2] // LANES), axis=1)
    note_ref[...] = jnp.broadcast_to(words[None], note_ref.shape)
    logarithm = jnp.log2(jnp.maximum(energy, 1e-30))
    sample = jnp.round(4.0 * logarithm)
    level = jnp.exp2(sample[:1] * -0.125)
    power = jnp.floor(logarithm)
    bits = jnp.round(energy * jnp.exp2(23.0 - power))
    row = lax.broadcasted_iota(jnp.int32, (8, BLK), 0)
    below = jnp.where(row == 1, sample, jnp.where(row == 2, power, bits)).astype(jnp.int32)
    for i, code_ref in enumerate(code_refs):
        here = slice(i * group, (i + 1) * group)
        values = (keep_ref[here] + came_ref[here]) * level
        largest = jnp.max(jnp.abs(values), axis=1, keepdims=True)
        exponent = jnp.floor(8.0 * jnp.log2(jnp.maximum(largest, 1e-30)) + 0.01) + 1.0
        codes = jnp.round(values * (STEPS * jnp.exp2(exponent * -0.125))).astype(jnp.int32)
        code_ref[:half] = (codes[:half] & 0xFFFF) | lax.shift_left(codes[half:], 16)
        exponents = jnp.sum(jnp.where(square, exponent, 0.0), axis=0, keepdims=True)
        exponents = jnp.broadcast_to(exponents.astype(jnp.int32), (8, group))
        exponents = jnp.concatenate([exponents] * (BLK // group), axis=1)
        code_ref[half:] = jnp.where(row == 0, exponents, below)


def decode(code_ref, square):
    half = code_ref.shape[0] - 8
    words = code_ref[:half]
    codes = jnp.concatenate(
        [lax.shift_right_arithmetic(lax.shift_left(words, 16), 16), lax.shift_right_arithmetic(words, 16)],
        axis=0,
    )
    below = code_ref[half:].astype(f32)
    exponent = jnp.sum(jnp.where(square, below[:1, : 2 * half], 0.0), axis=1, keepdims=True)
    level = jnp.exp2(below[1:2] * 0.125)
    energy = below[3:4] * jnp.exp2(below[2:3] - 23.0)
    return codes.astype(f32) * (jnp.exp2(exponent * 0.125) * (1.0 / STEPS)) * level, energy


def three(values):
    high = values.astype(bf16)
    rest = values - high.astype(f32)
    middle = rest.astype(bf16)
    low = (rest - middle.astype(f32)).astype(bf16)
    return high, middle, low


def pick(selector, parts):
    high, middle, low = [jnp.dot(selector, part, preferred_element_type=f32) for part in parts]
    return high + (middle + low)


def finish(here_ref, keep_ref, came_ref, energy_ref, a_ref, b_ref, c_ref, flags_ref, info_ref, stack_ref, windows_ref):
    group = stack_ref.shape[0]
    square = diagonal(group)
    stack = keep_ref[...] + came_ref[...]
    energy = energy_ref[:1]
    for code_ref in (a_ref, b_ref, c_ref):
        values, more = decode(code_ref, square)
        stack = stack + values
        energy = energy + more
    stack = stack * (1.0 / jnp.sqrt(energy + epsilon))
    stack_ref[...] = stack
    info = info_ref[:, 0, :LANES]
    chips = info.shape[0]
    core, here = here_ref[1], here_ref[2]
    lanes = lax.broadcasted_iota(jnp.int32, info.shape, 1)
    second = lanes >= SLOT
    device = 2 * lax.broadcasted_iota(jnp.int32, info.shape, 0) + jnp.where(second, 1 - core, core)
    word = jnp.where(second, lanes - SLOT, lanes)
    start = jnp.sum(jnp.where((word == SLOT - 1) & (device < here), info, 0))
    found = jnp.sum(flags_ref[...])
    mine = (info >= start) & (info < start + found) & (word < 32)
    rank = jnp.where(mine, info - start + 1, 0)
    ranks = [jnp.sum(jnp.where(side, rank, 0), axis=1, keepdims=True) - 1 for side in (lanes < SLOT, second)]
    ranks = [jnp.where(core == 0, ranks[k], ranks[1 - k]) for k in range(2)]
    rank = jnp.concatenate(ranks, axis=0)
    flags = jnp.broadcast_to(flags_ref[...], (8, group)).astype(f32)
    earlier = lax.broadcasted_iota(jnp.int32, (group, group), 0) < lax.broadcasted_iota(
        jnp.int32, (group, group), 1
    )
    before = jnp.dot(flags.astype(bf16), earlier.astype(f32).astype(bf16), preferred_element_type=f32)
    before = jnp.where(flags > 0.5, before, -2.0)
    selector = jnp.broadcast_to(before[:1], (2 * chips, group)) == rank.astype(f32)
    windows = pick(selector.astype(f32).astype(bf16), three(stack))
    across = BLK // LANES
    for k in range(across):
        rows = pl.ds(k, windows.shape[0], stride=across)
        windows_ref[rows, :] = windows[:, k * LANES : (k + 1) * LANES]


def cross(here_ref, lags_ref, events_ref, info_ref, received_ref, out_ref, turned, products):
    info = info_ref[:, 0, :LANES]
    chips = info.shape[0]
    pairs = out_ref.shape[0]
    core = here_ref[1]
    counts = [jnp.where(core == k, info[:, SLOT - 1 : SLOT], info[:, LANES - 1 :]) for k in range(2)]
    rows = lax.broadcasted_iota(jnp.int32, (chips, 2 * chips), 0)
    lanes = lax.broadcasted_iota(jnp.int32, (chips, 2 * chips), 1)
    second = lanes >= chips
    chip = jnp.where(second, lanes - chips, lanes)
    earlier = jnp.where(rows < chip, counts[0] + counts[1], 0)
    earlier = earlier + jnp.where((rows == chip) & second, counts[0], 0)
    starts = jnp.sum(earlier, axis=0, keepdims=True)
    own = jnp.where(rows == chip, jnp.where(second, counts[1], counts[0]), 0)
    ends = starts + jnp.sum(own, axis=0, keepdims=True)
    square = diagonal(pairs)
    both = jnp.concatenate(
        [
            jnp.sum(jnp.where(square, events_ref[i : i + 1], 0), axis=1, keepdims=True)
            for i in range(2)
        ],
        axis=0,
    )
    selector = (starts <= both) & (both < ends)
    across = BLK // LANES
    received = [received_ref[pl.ds(k, 2 * chips, stride=across), :] for k in range(across)]
    picked = pick(selector.astype(f32).astype(bf16), three(jnp.concatenate(received, axis=1)))
    first, second = picked[:pairs], picked[pairs:]
    length = 2 * BLK
    nothing = jnp.zeros((pairs, BLK), f32)
    ahead = jnp.concatenate([first, nothing], axis=1)
    behind = jnp.concatenate([second, nothing], axis=1)

    def near(values):
        return jnp.concatenate([values[:, length - NLAG :], values[:, :BLK]], axis=1)

    for u in range(NLAG // 8):
        turned[u] = near(behind if u == 0 else left(behind, 8 * u))
    for p in range(pairs):
        shift = lax.rem(lags_ref[p] + length, length)
        moved = pltpu.roll(jnp.broadcast_to(ahead[p : p + 1], (8, length)), shift, 1)
        moved = near(pltpu.roll(moved, 0, 1, stride=1, stride_axis=0))
        for u in range(NLAG // 8):
            product = moved * turned[u, pl.ds(p, 1), :]
            part = product[:, :LANES]
            for k in range(LANES, NLAG + BLK, LANES):
                part = part + product[:, k : k + LANES]
            products[pl.ds(p * NLAG + 8 * u, 8), :] = part
    ones = jnp.ones((8, LANES), bf16)
    high, middle, _ = three(products[...])
    high, middle = [
        lax.dot_general(ones, part, (((1,), (1,)), ((), ())), preferred_element_type=f32)
        for part in (high, middle)
    ]
    raw = high + middle
    raw = jnp.concatenate([raw[:1, p * NLAG : (p + 1) * NLAG] for p in range(pairs)], axis=0)
    power_one = jnp.mean(first * first, axis=1, keepdims=True)
    power_two = jnp.mean(second * second, axis=1, keepdims=True)
    out_ref[...] = raw / jnp.sqrt(BLK * (power_one + epsilon) * (power_two + epsilon))


def shards(waveforms, templates, detection_flags, pair_events, pair_lags):
    ahead, planes = lax.axis_size("tm"), lax.axis_size("z")
    chips = ahead * planes
    group = detection_flags.shape[0]
    plane, core = lax.axis_index("z"), lax.axis_index("core")
    place = (lax.axis_index("tm") * planes + plane) * 2 + core

    following = lax.ppermute(waveforms, "tm", [(i, i - 1) for i in range(1, ahead)])
    here = jnp.stack([plane, core, place, jnp.int32(planes)]).astype(jnp.int32)
    flags = detection_flags.reshape(1, group)
    events = pair_events.T
    words, waves = whole(
        announce,
        (pltpu.VMEM((8, LANES), f32), pltpu.VMEM(waveforms.shape, bf16)),
        1 << 20,
        waveforms,
        flags,
        events,
    )

    stations = templates.shape[1]

    def partial(distances, here, below):
        count = len(distances)
        flops = 4 * count * group * stations * TLEN * BLK
        shape = pltpu.VMEM((count * group + below, BLK), f32)
        return pl.pallas_call(
            functools.partial(correlate, distances),
            out_shape=(shape, shape),
            in_specs=[SMEM] + [pl.BlockSpec(memory_space=pl.ANY)] * 2 + [VMEM, pl.BlockSpec(memory_space=pltpu.HBM)],
            out_specs=(VMEM, VMEM),
            scratch_shapes=[
                pltpu.VMEM((2, stations, BLK), bf16),
                pltpu.VMEM((count, 2, group, stations, TLEN), bf16),
                pltpu.VMEM((stations * TLEN, BLK), bf16),
                pltpu.SemaphoreType.DMA((count + 1, 2)),
            ],
            compiler_params=pltpu.CompilerParams(vmem_limit_bytes=48 << 20),
            cost_estimate=pl.CostEstimate(
                flops=flops, bytes_accessed=flops // BLK, transcendentals=0
            ),
        )(here, waves, following, words, templates)

    def over(distance, values):
        return lax.ppermute(values, "z", [(i, (i + distance) % planes) for i in range(planes)])

    def swap(values):
        return lax.ppermute(values, "core", [(0, 1), (1, 0)])

    away = (2, 1, 3)
    keeps, sends = partial(away, here, 8)
    cames = swap(sends)
    later, _ = lax.optimization_barrier((here, keeps))
    keep, send = partial((0,), later, 0)
    came = swap(send)
    cames, _ = lax.optimization_barrier((cames, keep))
    shape = jax.ShapeDtypeStruct((group // 2 + 8, BLK), jnp.int32)
    note = jax.ShapeDtypeStruct((chips, 1, LANES), jnp.int32)
    energy, note, *codes = whole(
        merge,
        (jax.ShapeDtypeStruct((8, BLK), f32), note) + (shape,) * len(away),
        1 << 22,
        keeps,
        cames,
    )
    arrived = [over(distance, values) for distance, values in zip(away, codes)]
    info = lax.all_to_all(note, ("tm", "z"), 0, 0, tiled=True)

    network_stack, windows = whole(
        finish,
        (jax.ShapeDtypeStruct((group, BLK), f32), jax.ShapeDtypeStruct((2 * chips * BLK // LANES, LANES), f32)),
        1 << 24,
        here,
        keep,
        came,
        energy,
        *arrived,
        flags,
        info,
        smem=1,
    )
    windows = windows.reshape(2 * chips, BLK // LANES, LANES)
    received = lax.all_to_all(windows, ("core", "tm", "z"), 0, 0, tiled=True)
    received = received.reshape(-1, LANES)
    pairs = pair_events.shape[0]
    pair_cc = whole(
        cross,
        jax.ShapeDtypeStruct((pairs, NLAG), f32),
        1 << 24,
        here,
        pair_lags,
        events,
        info,
        received,
        smem=2,
        scratch=[
            pltpu.VMEM((NLAG // 8, pairs, NLAG + BLK), f32),
            pltpu.VMEM((pairs * NLAG, LANES), f32),
        ],
    )
    return (network_stack, pair_cc)


def solution(mesh):
    ahead, across = mesh.devices.shape
    split = jax.sharding.Mesh(mesh.devices.reshape(ahead, across // 2, 2), ("tm", "z", "core"))
    stations = ("z", "core")
    owners = ("tm", "z", "core")
    return jax.shard_map(
        shards,
        mesh=split,
        in_specs=(
            P(stations, "tm"),
            P(None, stations, None),
            P(stations, "tm"),
            P(owners, None),
            P(owners),
        ),
        out_specs=(P(stations, "tm"), P(owners, None)),
        check_vma=False,
    )
```

```python
import functools

import jax
import jax.numpy as jnp
from jax import lax
from jax.experimental import pallas as pl
from jax.experimental.pallas import tpu as pltpu
from jax.sharding import PartitionSpec as P

BLK = 512
TLEN = 512
NLAG = 128
LANES = 128
SLOT = 64
WORDS = 4
STEPS = 32767.0
epsilon = 1e-06
VMEM = pl.BlockSpec(memory_space=pltpu.VMEM)
SMEM = pl.BlockSpec(memory_space=pltpu.SMEM)
f32 = jnp.float32
bf16 = jnp.bfloat16


def whole(kernel, outs, flops, *operands, smem=0, scratch=()):
    return pl.pallas_call(
        kernel,
        out_shape=outs,
        in_specs=[SMEM] * smem + [VMEM] * (len(operands) - smem),
        out_specs=jax.tree.map(lambda _: VMEM, outs),
        scratch_shapes=scratch,
        compiler_params=pltpu.CompilerParams(vmem_limit_bytes=20 << 20),
        cost_estimate=pl.CostEstimate(flops=flops, bytes_accessed=1 << 20, transcendentals=0),
    )(*operands)


def left(values, distance):
    return pltpu.roll(values, values.shape[-1] - distance, values.ndim - 1)


def build(segment, sliding_ref):
    stations, length = segment.shape
    down = lax.broadcasted_iota(jnp.int32, (LANES, LANES), 0)
    along = lax.broadcasted_iota(jnp.int32, (LANES, LANES), 1)
    flip = (down + along == LANES - 1).astype(f32).astype(bf16)
    for s in range(stations):
        row = jnp.broadcast_to(segment[s : s + 1], (LANES, length))
        moved = pltpu.roll(row, length - LANES + 1, 1, stride=1, stride_axis=0).astype(bf16)
        shifted = jnp.dot(flip, moved, preferred_element_type=f32).astype(bf16)
        for k in range(0, TLEN, LANES):
            sliding_ref[pl.ds(s * TLEN + k, LANES), :] = shifted[:, k : k + BLK]


def announce(wave_ref, flags_ref, events_ref, words_ref, held_ref):
    held_ref[...] = wave_ref[...]
    fill = jnp.zeros((2, LANES - events_ref.shape[1]), f32)
    words = jnp.concatenate([events_ref[...].astype(f32), fill], axis=1)
    words = words[0:1] + pltpu.roll(words, events_ref.shape[1], 1)[1:2]
    count = jnp.sum(flags_ref[...].astype(f32), axis=1, keepdims=True)
    lane = lax.broadcasted_iota(jnp.int32, words.shape, 1)
    words_ref[...] = jnp.broadcast_to(jnp.where(lane == SLOT - 1, count, words), words_ref.shape)


def sums_of_window(squares):
    window = jnp.broadcast_to(squares, (8, squares.shape[1]))
    width = 1
    while width < TLEN:
        window = window + left(window, width)
        width *= 2
    return window[:, :BLK]


def correlate(distances, here_ref, wave_ref, next_ref, words_ref, templates_ref, keep_ref, send_ref, sliding, own, waves, held, arrival):
    planes = len(distances)
    group = held.shape[2]
    plane, core, around = here_ref[0], here_ref[1], here_ref[3]

    def copy(i, half):
        chip = lax.rem(plane + distances[i], around) if i < planes else plane
        first = (chip * 2 + (1 - core if half == 0 else core)) * group
        target = held.at[i, half] if i < planes else own.at[half]
        return pltpu.make_async_copy(templates_ref.at[pl.ds(first, group)], target, arrival.at[i, half])

    pieces = [
        pltpu.make_async_copy(wave_ref, waves.at[0], arrival.at[planes + 1, 0]),
        pltpu.make_async_copy(next_ref, waves.at[1], arrival.at[planes + 1, 1]),
    ]
    for piece in pieces:
        piece.start()
    for i in range(planes + 1):
        for half in range(2):
            copy(i, half).start()
    for piece in pieces:
        piece.wait()
    segment = jnp.concatenate([waves[0], waves[1]], axis=1).astype(f32)
    build(segment, sliding)
    energy = sums_of_window(jnp.sum(segment * segment, axis=0, keepdims=True))
    words = jnp.concatenate([words_ref[...]] * (BLK // LANES), axis=1)
    row = lax.broadcasted_iota(jnp.int32, energy.shape, 0)
    below = jnp.where(row == WORDS, words, energy)
    keep_ref[planes * group :] = below
    send_ref[planes * group :] = below
    for i in range(planes):
        for half, out_ref in enumerate((send_ref, keep_ref)):
            copy(i, half).wait()
            filters = held[i, half].reshape(group, -1)
            out_ref[i * group : (i + 1) * group] = jnp.dot(
                filters, sliding[...], preferred_element_type=f32
            )
    for half in range(2):
        copy(planes, half).wait()


def correlate_own(own_ref, sliding_ref, keep_ref, send_ref):
    for half, out_ref in enumerate((send_ref, keep_ref)):
        filters = own_ref[half].reshape(own_ref.shape[1], -1)
        out_ref[...] = jnp.dot(filters, sliding_ref[...], preferred_element_type=f32)


def diagonal(size):
    rows = lax.broadcasted_iota(jnp.int32, (size, size), 0)
    return rows == lax.broadcasted_iota(jnp.int32, (size, size), 1)


def merge(keep_ref, came_ref, energy_ref, note_ref, *code_refs):
    half = code_refs[0].shape[0] - 8
    group = 2 * half
    square = diagonal(group)
    last = len(code_refs) * group
    energy = keep_ref[last:] + came_ref[last:]
    energy_ref[...] = energy
    words = [ref[last + WORDS : last + WORDS + 1, :LANES].astype(jnp.int32) for ref in (keep_ref, came_ref)]
    lane = lax.broadcasted_iota(jnp.int32, (1, LANES), 1)
    words = jnp.where(lane < SLOT, words[0], pltpu.roll(words[1], SLOT, 1))
    words = jnp.concatenate([words] * (note_ref.shape[2] // LANES), axis=1)
    note_ref[...] = jnp.broadcast_to(words[None], note_ref.shape)
    logarithm = jnp.log2(jnp.maximum(energy, 1e-30))
    sample = jnp.round(4.0 * logarithm)
    level = jnp.exp2(sample[:1] * -0.125)
    power = jnp.floor(logarithm)
    bits = jnp.round(energy * jnp.exp2(23.0 - power))
    row = lax.broadcasted_iota(jnp.int32, (8, BLK), 0)
    below = jnp.where(row == 1, sample, jnp.where(row == 2, power, bits)).astype(jnp.int32)
    for i, code_ref in enumerate(code_refs):
        here = slice(i * group, (i + 1) * group)
        values = (keep_ref[here] + came_ref[here]) * level
        largest = jnp.max(jnp.abs(values), axis=1, keepdims=True)
        exponent = jnp.floor(8.0 * jnp.log2(jnp.maximum(largest, 1e-30)) + 0.01) + 1.0
        codes = jnp.round(values * (STEPS * jnp.exp2(exponent * -0.125))).astype(jnp.int32)
        code_ref[:half] = (codes[:half] & 0xFFFF) | lax.shift_left(codes[half:], 16)
        exponents = jnp.sum(jnp.where(square, exponent, 0.0), axis=0, keepdims=True)
        exponents = jnp.broadcast_to(exponents.astype(jnp.int32), (8, group))
        exponents = jnp.concatenate([exponents] * (BLK // group), axis=1)
        code_ref[half:] = jnp.where(row == 0, exponents, below)


def decode(code_ref, square):
    half = code_ref.shape[0] - 8
    words = code_ref[:half]
    codes = jnp.concatenate(
        [lax.shift_right_arithmetic(lax.shift_left(words, 16), 16), lax.shift_right_arithmetic(words, 16)],
        axis=0,
    )
    below = code_ref[half:].astype(f32)
    exponent = jnp.sum(jnp.where(square, below[:1, : 2 * half], 0.0), axis=1, keepdims=True)
    level = jnp.exp2(below[1:2] * 0.125)
    energy = below[3:4] * jnp.exp2(below[2:3] - 23.0)
    return codes.astype(f32) * (jnp.exp2(exponent * 0.125) * (1.0 / STEPS)) * level, energy


def three(values):
    high = values.astype(bf16)
    rest = values - high.astype(f32)
    middle = rest.astype(bf16)
    low = (rest - middle.astype(f32)).astype(bf16)
    return high, middle, low


def pick(selector, parts):
    high, middle, low = [jnp.dot(selector, part, preferred_element_type=f32) for part in parts]
    return high + (middle + low)


def finish(here_ref, keep_ref, came_ref, energy_ref, a_ref, b_ref, c_ref, flags_ref, info_ref, stack_ref, windows_ref):
    group = stack_ref.shape[0]
    square = diagonal(group)
    stack = keep_ref[...] + came_ref[...]
    energy = energy_ref[:1]
    for code_ref in (a_ref, b_ref, c_ref):
        values, more = decode(code_ref, square)
        stack = stack + values
        energy = energy + more
    stack = stack * (1.0 / jnp.sqrt(energy + epsilon))
    stack_ref[...] = stack
    info = info_ref[:, 0, :LANES]
    chips = info.shape[0]
    core, here = here_ref[1], here_ref[2]
    lanes = lax.broadcasted_iota(jnp.int32, info.shape, 1)
    second = lanes >= SLOT
    device = 2 * lax.broadcasted_iota(jnp.int32, info.shape, 0) + jnp.where(second, 1 - core, core)
    word = jnp.where(second, lanes - SLOT, lanes)
    start = jnp.sum(jnp.where((word == SLOT - 1) & (device < here), info, 0))
    found = jnp.sum(flags_ref[...])
    mine = (info >= start) & (info < start + found) & (word < 32)
    rank = jnp.where(mine, info - start + 1, 0)
    ranks = [jnp.sum(jnp.where(side, rank, 0), axis=1, keepdims=True) - 1 for side in (lanes < SLOT, second)]
    ranks = [jnp.where(core == 0, ranks[k], ranks[1 - k]) for k in range(2)]
    rank = jnp.concatenate(ranks, axis=0)
    flags = jnp.broadcast_to(flags_ref[...], (8, group)).astype(f32)
    earlier = lax.broadcasted_iota(jnp.int32, (group, group), 0) < lax.broadcasted_iota(
        jnp.int32, (group, group), 1
    )
    before = jnp.dot(flags.astype(bf16), earlier.astype(f32).astype(bf16), preferred_element_type=f32)
    before = jnp.where(flags > 0.5, before, -2.0)
    selector = jnp.broadcast_to(before[:1], (2 * chips, group)) == rank.astype(f32)
    windows = pick(selector.astype(f32).astype(bf16), three(stack))
    across = BLK // LANES
    for k in range(across):
        rows = pl.ds(k, windows.shape[0], stride=across)
        windows_ref[rows, :] = windows[:, k * LANES : (k + 1) * LANES]


def cross(here_ref, lags_ref, events_ref, info_ref, received_ref, out_ref, turned, products):
    info = info_ref[:, 0, :LANES]
    chips = info.shape[0]
    pairs = out_ref.shape[0]
    core = here_ref[1]
    counts = [jnp.where(core == k, info[:, SLOT - 1 : SLOT], info[:, LANES - 1 :]) for k in range(2)]
    rows = lax.broadcasted_iota(jnp.int32, (chips, 2 * chips), 0)
    lanes = lax.broadcasted_iota(jnp.int32, (chips, 2 * chips), 1)
    second = lanes >= chips
    chip = jnp.where(second, lanes - chips, lanes)
    earlier = jnp.where(rows < chip, counts[0] + counts[1], 0)
    earlier = earlier + jnp.where((rows == chip) & second, counts[0], 0)
    starts = jnp.sum(earlier, axis=0, keepdims=True)
    own = jnp.where(rows == chip, jnp.where(second, counts[1], counts[0]), 0)
    ends = starts + jnp.sum(own, axis=0, keepdims=True)
    square = diagonal(pairs)
    both = jnp.concatenate(
        [
            jnp.sum(jnp.where(square, events_ref[i : i + 1], 0), axis=1, keepdims=True)
            for i in range(2)
        ],
        axis=0,
    )
    selector = (starts <= both) & (both < ends)
    across = BLK // LANES
    received = [received_ref[pl.ds(k, 2 * chips, stride=across), :] for k in range(across)]
    picked = pick(selector.astype(f32).astype(bf16), three(jnp.concatenate(received, axis=1)))
    first, second = picked[:pairs], picked[pairs:]
    length = 2 * BLK
    nothing = jnp.zeros((pairs, BLK), f32)
    ahead = jnp.concatenate([first, nothing], axis=1)
    behind = jnp.concatenate([second, nothing], axis=1)

    def near(values):
        return jnp.concatenate([values[:, length - NLAG :], values[:, :BLK]], axis=1)

    for u in range(NLAG // 8):
        turned[u] = near(behind if u == 0 else left(behind, 8 * u))
    for p in range(pairs):
        shift = lax.rem(lags_ref[p] + length, length)
        moved = pltpu.roll(jnp.broadcast_to(ahead[p : p + 1], (8, length)), shift, 1)
        moved = near(pltpu.roll(moved, 0, 1, stride=1, stride_axis=0))
        for u in range(NLAG // 8):
            product = moved * turned[u, pl.ds(p, 1), :]
            part = product[:, :LANES]
            for k in range(LANES, NLAG + BLK, LANES):
                part = part + product[:, k : k + LANES]
            products[pl.ds(p * NLAG + 8 * u, 8), :] = part
    ones = jnp.ones((8, LANES), bf16)
    high, middle, _ = three(products[...])
    high, middle = [
        lax.dot_general(ones, part, (((1,), (1,)), ((), ())), preferred_element_type=f32)
        for part in (high, middle)
    ]
    raw = high + middle
    raw = jnp.concatenate([raw[:1, p * NLAG : (p + 1) * NLAG] for p in range(pairs)], axis=0)
    power_one = jnp.mean(first * first, axis=1, keepdims=True)
    power_two = jnp.mean(second * second, axis=1, keepdims=True)
    out_ref[...] = raw / jnp.sqrt(BLK * (power_one + epsilon) * (power_two + epsilon))


def shards(waveforms, templates, detection_flags, pair_events, pair_lags):
    ahead, planes = lax.axis_size("tm"), lax.axis_size("z")
    chips = ahead * planes
    group = detection_flags.shape[0]
    plane, core = lax.axis_index("z"), lax.axis_index("core")
    place = (lax.axis_index("tm") * planes + plane) * 2 + core

    following = lax.ppermute(waveforms, "tm", [(i, i - 1) for i in range(1, ahead)])
    here = jnp.stack([plane, core, place, jnp.int32(planes)]).astype(jnp.int32)
    flags = detection_flags.reshape(1, group)
    events = pair_events.T
    words, waves = whole(
        announce,
        (pltpu.VMEM((8, LANES), f32), pltpu.VMEM(waveforms.shape, bf16)),
        1 << 20,
        waveforms,
        flags,
        events,
    )

    stations = templates.shape[1]
    away = (2, 1, 3)
    any_space = pl.BlockSpec(memory_space=pl.ANY)
    flops = 4 * group * stations * TLEN * BLK
    shape = pltpu.VMEM((len(away) * group + 8, BLK), f32)
    keeps, sends, sliding, own = pl.pallas_call(
        functools.partial(correlate, away),
        out_shape=(
            shape,
            shape,
            pltpu.VMEM((stations * TLEN, BLK), bf16),
            pltpu.VMEM((2, group, stations, TLEN), bf16),
        ),
        in_specs=[SMEM, any_space, any_space, VMEM, pl.BlockSpec(memory_space=pltpu.HBM)],
        out_specs=(VMEM,) * 4,
        scratch_shapes=[
            pltpu.VMEM((2, stations, BLK), bf16),
            pltpu.VMEM((len(away), 2, group, stations, TLEN), bf16),
            pltpu.SemaphoreType.DMA((len(away) + 2, 2)),
        ],
        compiler_params=pltpu.CompilerParams(vmem_limit_bytes=42 << 20),
        cost_estimate=pl.CostEstimate(
            flops=len(away) * flops, bytes_accessed=len(away) * flops // BLK, transcendentals=0
        ),
    )(here, waves, following, words, templates)

    def over(distance, values):
        return lax.ppermute(values, "z", [(i, (i + distance) % planes) for i in range(planes)])

    def swap(values):
        return lax.ppermute(values, "core", [(0, 1), (1, 0)])

    cames = swap(sends)
    shape = pltpu.VMEM((group, BLK), f32)
    keep, send = whole(correlate_own, (shape, shape), flops, own, sliding)
    came = swap(send)
    cames, _ = lax.optimization_barrier((cames, keep))
    shape = jax.ShapeDtypeStruct((group // 2 + 8, BLK), jnp.int32)
    note = jax.ShapeDtypeStruct((chips, 1, LANES), jnp.int32)
    energy, note, *codes = whole(
        merge,
        (jax.ShapeDtypeStruct((8, BLK), f32), note) + (shape,) * len(away),
        1 << 22,
        keeps,
        cames,
    )
    arrived = [over(distance, values) for distance, values in zip(away, codes)]
    info = lax.all_to_all(note, ("tm", "z"), 0, 0, tiled=True)

    network_stack, windows = whole(
        finish,
        (pltpu.VMEM((group, BLK), f32), jax.ShapeDtypeStruct((2 * chips * BLK // LANES, LANES), f32)),
        1 << 24,
        here,
        keep,
        came,
        energy,
        *arrived,
        flags,
        info,
        smem=1,
    )
    windows = windows.reshape(2 * chips, BLK // LANES, LANES)
    received = lax.all_to_all(windows, ("core", "tm", "z"), 0, 0, tiled=True)
    received = received.reshape(-1, LANES)
    pairs = pair_events.shape[0]
    pair_cc = whole(
        cross,
        jax.ShapeDtypeStruct((pairs, NLAG), f32),
        1 << 24,
        here,
        pair_lags,
        events,
        info,
        received,
        smem=2,
        scratch=[
            pltpu.VMEM((NLAG // 8, pairs, NLAG + BLK), f32),
            pltpu.VMEM((pairs * NLAG, LANES), f32),
        ],
    )
    return (network_stack, pair_cc)


def solution(mesh):
    ahead, across = mesh.devices.shape
    split = jax.sharding.Mesh(mesh.devices.reshape(ahead, across // 2, 2), ("tm", "z", "core"))
    stations = ("z", "core")
    owners = ("tm", "z", "core")
    return jax.shard_map(
        shards,
        mesh=split,
        in_specs=(
            P(stations, "tm"),
            P(None, stations, None),
            P(stations, "tm"),
            P(owners, None),
            P(owners),
        ),
        out_specs=(P(stations, "tm"), P(owners, None)),
        check_vma=False,
    )
```

```python
import functools

import jax
import jax.numpy as jnp
from jax import lax
from jax.experimental import pallas as pl
from jax.experimental.pallas import tpu as pltpu
from jax.sharding import PartitionSpec as P

BLK = 512
TLEN = 512
NLAG = 128
LANES = 128
SLOT = 64
WORDS = 4
STEPS = 32767.0
epsilon = 1e-06
VMEM = pl.BlockSpec(memory_space=pltpu.VMEM)
SMEM = pl.BlockSpec(memory_space=pltpu.SMEM)
f32 = jnp.float32
bf16 = jnp.bfloat16


def whole(kernel, outs, flops, *operands, smem=0, scratch=()):
    return pl.pallas_call(
        kernel,
        out_shape=outs,
        in_specs=[SMEM] * smem + [VMEM] * (len(operands) - smem),
        out_specs=jax.tree.map(lambda _: VMEM, outs),
        scratch_shapes=scratch,
        compiler_params=pltpu.CompilerParams(vmem_limit_bytes=20 << 20),
        cost_estimate=pl.CostEstimate(flops=flops, bytes_accessed=1 << 20, transcendentals=0),
    )(*operands)


def left(values, distance):
    return pltpu.roll(values, values.shape[-1] - distance, values.ndim - 1)


def build(segment, sliding_ref):
    stations, length = segment.shape
    down = lax.broadcasted_iota(jnp.int32, (LANES, LANES), 0)
    along = lax.broadcasted_iota(jnp.int32, (LANES, LANES), 1)
    flip = (down + along == LANES - 1).astype(f32).astype(bf16)
    for s in range(stations):
        row = jnp.broadcast_to(segment[s : s + 1], (LANES, length))
        moved = pltpu.roll(row, length - LANES + 1, 1, stride=1, stride_axis=0).astype(bf16)
        shifted = jnp.dot(flip, moved, preferred_element_type=f32).astype(bf16)
        for k in range(0, TLEN, LANES):
            sliding_ref[pl.ds(s * TLEN + k, LANES), :] = shifted[:, k : k + BLK]


def announce(wave_ref, flags_ref, events_ref, words_ref, held_ref):
    held_ref[...] = wave_ref[...]
    fill = jnp.zeros((2, LANES - events_ref.shape[1]), f32)
    words = jnp.concatenate([events_ref[...].astype(f32), fill], axis=1)
    words = words[0:1] + pltpu.roll(words, events_ref.shape[1], 1)[1:2]
    count = jnp.sum(flags_ref[...].astype(f32), axis=1, keepdims=True)
    lane = lax.broadcasted_iota(jnp.int32, words.shape, 1)
    words_ref[...] = jnp.broadcast_to(jnp.where(lane == SLOT - 1, count, words), words_ref.shape)


def sums_of_window(squares):
    window = jnp.broadcast_to(squares, (8, squares.shape[1]))
    width = 1
    while width < TLEN:
        window = window + left(window, width)
        width *= 2
    return window[:, :BLK]


def correlate(distances, here_ref, wave_ref, next_ref, words_ref, templates_ref, keep_ref, send_ref, sliding, own, waves, held, arrival):
    planes = len(distances)
    group = held.shape[2]
    plane, core, around = here_ref[0], here_ref[1], here_ref[3]

    def copy(i, half):
        chip = lax.rem(plane + distances[i], around) if i < planes else plane
        first = (chip * 2 + (1 - core if half == 0 else core)) * group
        target = held.at[i, half] if i < planes else own.at[half]
        return pltpu.make_async_copy(templates_ref.at[pl.ds(first, group)], target, arrival.at[i, half])

    pieces = [
        pltpu.make_async_copy(wave_ref, waves.at[0], arrival.at[planes + 1, 0]),
        pltpu.make_async_copy(next_ref, waves.at[1], arrival.at[planes + 1, 1]),
    ]
    for piece in pieces:
        piece.start()
    for i in range(planes + 1):
        for half in range(2):
            copy(i, half).start()
    for piece in pieces:
        piece.wait()
    segment = jnp.concatenate([waves[0], waves[1]], axis=1).astype(f32)
    build(segment, sliding)
    energy = sums_of_window(jnp.sum(segment * segment, axis=0, keepdims=True))
    words = jnp.concatenate([words_ref[...]] * (BLK // LANES), axis=1)
    row = lax.broadcasted_iota(jnp.int32, energy.shape, 0)
    below = jnp.where(row == WORDS, words, energy)
    keep_ref[planes * group :] = below
    send_ref[planes * group :] = below
    for i in range(planes):
        for half, out_ref in enumerate((send_ref, keep_ref)):
            copy(i, half).wait()
            filters = held[i, half].reshape(group, -1)
            out_ref[i * group : (i + 1) * group] = jnp.dot(
                filters, sliding[...], preferred_element_type=f32
            )
    for half in range(2):
        copy(planes, half).wait()


def correlate_own(own_ref, sliding_ref, keep_ref, send_ref):
    for half, out_ref in enumerate((send_ref, keep_ref)):
        filters = own_ref[half].reshape(own_ref.shape[1], -1)
        out_ref[...] = jnp.dot(filters, sliding_ref[...], preferred_element_type=f32)


def diagonal(size):
    rows = lax.broadcasted_iota(jnp.int32, (size, size), 0)
    return rows == lax.broadcasted_iota(jnp.int32, (size, size), 1)


def merge(keep_ref, came_ref, energy_ref, note_ref, *code_refs):
    half = code_refs[0].shape[0] - 8
    group = 2 * half
    square = diagonal(group)
    last = len(code_refs) * group
    energy = keep_ref[last:] + came_ref[last:]
    energy_ref[...] = energy
    words = [ref[last + WORDS : last + WORDS + 1, :LANES].astype(jnp.int32) for ref in (keep_ref, came_ref)]
    lane = lax.broadcasted_iota(jnp.int32, (1, LANES), 1)
    words = jnp.where(lane < SLOT, words[0], pltpu.roll(words[1], SLOT, 1))
    note_ref[...] = jnp.broadcast_to(words, note_ref.shape)
    logarithm = jnp.log2(jnp.maximum(energy, 1e-30))
    sample = jnp.round(4.0 * logarithm)
    level = jnp.exp2(sample[:1] * -0.125)
    power = jnp.floor(logarithm)
    bits = jnp.round(energy * jnp.exp2(23.0 - power))
    row = lax.broadcasted_iota(jnp.int32, (8, BLK), 0)
    below = jnp.where(row == 1, sample, jnp.where(row == 2, power, bits)).astype(jnp.int32)
    for i, code_ref in enumerate(code_refs):
        here = slice(i * group, (i + 1) * group)
        values = (keep_ref[here] + came_ref[here]) * level
        largest = jnp.max(jnp.abs(values), axis=1, keepdims=True)
        exponent = jnp.floor(8.0 * jnp.log2(jnp.maximum(largest, 1e-30)) + 0.01) + 1.0
        codes = jnp.round(values * (STEPS * jnp.exp2(exponent * -0.125))).astype(jnp.int32)
        code_ref[:half] = (codes[:half] & 0xFFFF) | lax.shift_left(codes[half:], 16)
        exponents = jnp.sum(jnp.where(square, exponent, 0.0), axis=0, keepdims=True)
        exponents = jnp.broadcast_to(exponents.astype(jnp.int32), (8, group))
        exponents = jnp.concatenate([exponents] * (BLK // group), axis=1)
        code_ref[half:] = jnp.where(row == 0, exponents, below)


def decode(code_ref, square):
    half = code_ref.shape[0] - 8
    words = code_ref[:half]
    codes = jnp.concatenate(
        [lax.shift_right_arithmetic(lax.shift_left(words, 16), 16), lax.shift_right_arithmetic(words, 16)],
        axis=0,
    )
    below = code_ref[half:].astype(f32)
    exponent = jnp.sum(jnp.where(square, below[:1, : 2 * half], 0.0), axis=1, keepdims=True)
    level = jnp.exp2(below[1:2] * 0.125)
    energy = below[3:4] * jnp.exp2(below[2:3] - 23.0)
    return codes.astype(f32) * (jnp.exp2(exponent * 0.125) * (1.0 / STEPS)) * level, energy


def three(values):
    high = values.astype(bf16)
    rest = values - high.astype(f32)
    middle = rest.astype(bf16)
    low = (rest - middle.astype(f32)).astype(bf16)
    return high, middle, low


def pick(selector, parts):
    high, middle, low = [jnp.dot(selector, part, preferred_element_type=f32) for part in parts]
    return high + (middle + low)


def finish(keep_ref, came_ref, energy_ref, a_ref, b_ref, c_ref, flags_ref, stack_ref, parts_ref, before_ref, found_ref):
    group = stack_ref.shape[0]
    square = diagonal(group)
    stack = keep_ref[...] + came_ref[...]
    energy = energy_ref[:1]
    for code_ref in (a_ref, b_ref, c_ref):
        values, more = decode(code_ref, square)
        stack = stack + values
        energy = energy + more
    stack = stack * (1.0 / jnp.sqrt(energy + epsilon))
    stack_ref[...] = stack
    for i, part in enumerate(three(stack)):
        parts_ref[i] = part
    flags = jnp.broadcast_to(flags_ref[...], (8, group)).astype(f32)
    earlier = lax.broadcasted_iota(jnp.int32, (group, group), 0) < lax.broadcasted_iota(
        jnp.int32, (group, group), 1
    )
    before = jnp.dot(flags.astype(bf16), earlier.astype(f32).astype(bf16), preferred_element_type=f32)
    before_ref[...] = jnp.where(flags > 0.5, before, -2.0)
    found = jnp.sum(flags_ref[...], axis=1, keepdims=True)
    found_ref[...] = jnp.broadcast_to(found, found_ref.shape)


def select(here_ref, parts_ref, before_ref, found_ref, info_ref, windows_ref):
    info = info_ref[...]
    chips = info.shape[0]
    core, here = here_ref[1], here_ref[2]
    lanes = lax.broadcasted_iota(jnp.int32, info.shape, 1)
    second = lanes >= SLOT
    device = 2 * lax.broadcasted_iota(jnp.int32, info.shape, 0) + jnp.where(second, 1 - core, core)
    word = jnp.where(second, lanes - SLOT, lanes)
    start = jnp.where((word == SLOT - 1) & (device < here), info, 0)
    start = jnp.sum(jnp.sum(start, axis=0, keepdims=True), axis=1, keepdims=True)
    found = found_ref[:1, :1]
    mine = (info >= start) & (info < start + found) & (word < 32)
    rank = jnp.where(mine, info - start + 1, 0)
    ranks = [jnp.sum(jnp.where(side, rank, 0), axis=1, keepdims=True) - 1 for side in (lanes < SLOT, second)]
    ranks = [jnp.where(core == 0, ranks[k], ranks[1 - k]) for k in range(2)]
    rank = jnp.concatenate(ranks, axis=0)
    before = jnp.broadcast_to(before_ref[:1], (2 * chips, before_ref.shape[1]))
    selector = before == rank.astype(f32)
    windows = pick(selector.astype(f32).astype(bf16), [parts_ref[i] for i in range(3)])
    across = BLK // LANES
    for k in range(across):
        rows = pl.ds(k, windows.shape[0], stride=across)
        windows_ref[rows, :] = windows[:, k * LANES : (k + 1) * LANES]


def choose(here_ref, events_ref, info_ref, selector_ref):
    info = info_ref[...]
    chips = info.shape[0]
    pairs = events_ref.shape[1]
    core = here_ref[1]
    counts = [jnp.where(core == k, info[:, SLOT - 1 : SLOT], info[:, LANES - 1 :]) for k in range(2)]
    rows = lax.broadcasted_iota(jnp.int32, (chips, 2 * chips), 0)
    lanes = lax.broadcasted_iota(jnp.int32, (chips, 2 * chips), 1)
    second = lanes >= chips
    chip = jnp.where(second, lanes - chips, lanes)
    earlier = jnp.where(rows < chip, counts[0] + counts[1], 0)
    earlier = earlier + jnp.where((rows == chip) & second, counts[0], 0)
    starts = jnp.sum(earlier, axis=0, keepdims=True)
    own = jnp.where(rows == chip, jnp.where(second, counts[1], counts[0]), 0)
    ends = starts + jnp.sum(own, axis=0, keepdims=True)
    square = diagonal(pairs)
    both = jnp.concatenate(
        [
            jnp.sum(jnp.where(square, events_ref[i : i + 1], 0), axis=1, keepdims=True)
            for i in range(2)
        ],
        axis=0,
    )
    selector_ref[...] = ((starts <= both) & (both < ends)).astype(f32)


def cross(lags_ref, selector_ref, received_ref, out_ref, turned, products):
    pairs = out_ref.shape[0]
    across = BLK // LANES
    sources = selector_ref.shape[1]
    received = [received_ref[pl.ds(k, sources, stride=across), :] for k in range(across)]
    picked = pick(selector_ref[...].astype(bf16), three(jnp.concatenate(received, axis=1)))
    first, second = picked[:pairs], picked[pairs:]
    length = 2 * BLK
    nothing = jnp.zeros((pairs, BLK), f32)
    ahead = jnp.concatenate([first, nothing], axis=1)
    behind = jnp.concatenate([second, nothing], axis=1)

    def near(values):
        return jnp.concatenate([values[:, length - NLAG :], values[:, :BLK]], axis=1)

    for u in range(NLAG // 8):
        turned[u] = near(behind if u == 0 else left(behind, 8 * u))
    for p in range(pairs):
        shift = lax.rem(lags_ref[p] + length, length)
        moved = pltpu.roll(jnp.broadcast_to(ahead[p : p + 1], (8, length)), shift, 1)
        moved = near(pltpu.roll(moved, 0, 1, stride=1, stride_axis=0))
        for u in range(NLAG // 8):
            product = moved * turned[u, pl.ds(p, 1), :]
            part = product[:, :LANES]
            for k in range(LANES, NLAG + BLK, LANES):
                part = part + product[:, k : k + LANES]
            products[pl.ds(p * NLAG + 8 * u, 8), :] = part
    ones = jnp.ones((8, LANES), bf16)
    high, middle, _ = three(products[...])
    high, middle = [
        lax.dot_general(ones, part, (((1,), (1,)), ((), ())), preferred_element_type=f32)
        for part in (high, middle)
    ]
    raw = high + middle
    raw = jnp.concatenate([raw[:1, p * NLAG : (p + 1) * NLAG] for p in range(pairs)], axis=0)
    power_one = jnp.mean(first * first, axis=1, keepdims=True)
    power_two = jnp.mean(second * second, axis=1, keepdims=True)
    out_ref[...] = raw / jnp.sqrt(BLK * (power_one + epsilon) * (power_two + epsilon))


def shards(waveforms, templates, detection_flags, pair_events, pair_lags):
    ahead, planes = lax.axis_size("tm"), lax.axis_size("z")
    chips = ahead * planes
    group = detection_flags.shape[0]
    plane, core = lax.axis_index("z"), lax.axis_index("core")
    place = (lax.axis_index("tm") * planes + plane) * 2 + core

    following = lax.ppermute(waveforms, "tm", [(i, i - 1) for i in range(1, ahead)])
    here = jnp.stack([plane, core, place, jnp.int32(planes)]).astype(jnp.int32)
    flags = detection_flags.reshape(1, group)
    events = pair_events.T
    words, waves = whole(
        announce,
        (pltpu.VMEM((8, LANES), f32), pltpu.VMEM(waveforms.shape, bf16)),
        1 << 20,
        waveforms,
        flags,
        events,
    )

    stations = templates.shape[1]
    away = (2, 1, 3)
    any_space = pl.BlockSpec(memory_space=pl.ANY)
    flops = 4 * group * stations * TLEN * BLK
    shape = pltpu.VMEM((len(away) * group + 8, BLK), f32)
    keeps, sends, sliding, own = pl.pallas_call(
        functools.partial(correlate, away),
        out_shape=(
            shape,
            shape,
            pltpu.VMEM((stations * TLEN, BLK), bf16),
            pltpu.VMEM((2, group, stations, TLEN), bf16),
        ),
        in_specs=[SMEM, any_space, any_space, VMEM, pl.BlockSpec(memory_space=pltpu.HBM)],
        out_specs=(VMEM,) * 4,
        scratch_shapes=[
            pltpu.VMEM((2, stations, BLK), bf16),
            pltpu.VMEM((len(away), 2, group, stations, TLEN), bf16),
            pltpu.SemaphoreType.DMA((len(away) + 2, 2)),
        ],
        compiler_params=pltpu.CompilerParams(vmem_limit_bytes=42 << 20),
        cost_estimate=pl.CostEstimate(
            flops=len(away) * flops, bytes_accessed=len(away) * flops // BLK, transcendentals=0
        ),
    )(here, waves, following, words, templates)

    def over(distance, values):
        return lax.ppermute(values, "z", [(i, (i + distance) % planes) for i in range(planes)])

    def swap(values):
        return lax.ppermute(values, "core", [(0, 1), (1, 0)])

    cames = swap(sends)
    shape = pltpu.VMEM((group, BLK), f32)
    keep, send = whole(correlate_own, (shape, shape), flops, own, sliding)
    came = swap(send)
    cames, _ = lax.optimization_barrier((cames, keep))
    shape = pltpu.VMEM((group // 2 + 8, BLK), jnp.int32)
    note = pltpu.VMEM((chips, LANES), jnp.int32)
    energy, note, *codes = whole(
        merge,
        (pltpu.VMEM((8, BLK), f32), note) + (shape,) * len(away),
        1 << 22,
        keeps,
        cames,
    )
    arrived = [over(distance, values) for distance, values in zip(away, codes)]
    info = lax.all_to_all(note.reshape(chips, 1, LANES), ("tm", "z"), 0, 0, tiled=True)
    info = info.reshape(chips, LANES)

    network_stack, parts, before, found = whole(
        finish,
        (
            pltpu.VMEM((group, BLK), f32),
            pltpu.VMEM((3, group, BLK), bf16),
            pltpu.VMEM((8, group), f32),
            pltpu.VMEM((8, LANES), jnp.int32),
        ),
        1 << 24,
        keep,
        came,
        energy,
        *arrived,
        flags,
    )
    windows = whole(
        select,
        pltpu.VMEM((2 * chips * BLK // LANES, LANES), f32),
        1 << 24,
        here,
        parts,
        before,
        found,
        info,
        smem=1,
    )
    windows = windows.reshape(2 * chips, BLK // LANES, LANES)
    received = lax.all_to_all(windows, ("core", "tm", "z"), 0, 0, tiled=True)
    received = received.reshape(-1, LANES)
    pairs = pair_events.shape[0]
    selector = whole(
        choose, pltpu.VMEM((2 * pairs, 2 * chips), f32), 1 << 20, here, events, info, smem=1
    )
    pair_cc = whole(
        cross,
        jax.ShapeDtypeStruct((pairs, NLAG), f32),
        1 << 24,
        pair_lags,
        selector,
        received,
        smem=1,
        scratch=[
            pltpu.VMEM((NLAG // 8, pairs, NLAG + BLK), f32),
            pltpu.VMEM((pairs * NLAG, LANES), f32),
        ],
    )
    return (network_stack, pair_cc)


def solution(mesh):
    ahead, across = mesh.devices.shape
    split = jax.sharding.Mesh(mesh.devices.reshape(ahead, across // 2, 2), ("tm", "z", "core"))
    stations = ("z", "core")
    owners = ("tm", "z", "core")
    return jax.shard_map(
        shards,
        mesh=split,
        in_specs=(
            P(stations, "tm"),
            P(None, stations, None),
            P(stations, "tm"),
            P(owners, None),
            P(owners),
        ),
        out_specs=(P(stations, "tm"), P(owners, None)),
        check_vma=False,
    )
```

```python
import functools

import jax
import jax.numpy as jnp
from jax import lax
from jax.experimental import pallas as pl
from jax.experimental.pallas import tpu as pltpu
from jax.sharding import PartitionSpec as P

BLK = 512
TLEN = 512
NLAG = 128
LANES = 128
SLOT = 64
WORDS = 4
STEPS = 32767.0
epsilon = 1e-06
VMEM = pl.BlockSpec(memory_space=pltpu.VMEM)
SMEM = pl.BlockSpec(memory_space=pltpu.SMEM)
f32 = jnp.float32
bf16 = jnp.bfloat16


def whole(kernel, outs, flops, *operands, smem=0, scratch=()):
    return pl.pallas_call(
        kernel,
        out_shape=outs,
        in_specs=[SMEM] * smem + [VMEM] * (len(operands) - smem),
        out_specs=jax.tree.map(lambda _: VMEM, outs),
        scratch_shapes=scratch,
        compiler_params=pltpu.CompilerParams(vmem_limit_bytes=20 << 20),
        cost_estimate=pl.CostEstimate(flops=flops, bytes_accessed=1 << 20, transcendentals=0),
    )(*operands)


def left(values, distance):
    return pltpu.roll(values, values.shape[-1] - distance, values.ndim - 1)


def build(segment, sliding_ref):
    stations, length = segment.shape
    down = lax.broadcasted_iota(jnp.int32, (LANES, LANES), 0)
    along = lax.broadcasted_iota(jnp.int32, (LANES, LANES), 1)
    flip = (down + along == LANES - 1).astype(f32).astype(bf16)
    for s in range(stations):
        row = jnp.broadcast_to(segment[s : s + 1], (LANES, length))
        moved = pltpu.roll(row, length - LANES + 1, 1, stride=1, stride_axis=0).astype(bf16)
        shifted = jnp.dot(flip, moved, preferred_element_type=f32).astype(bf16)
        for k in range(0, TLEN, LANES):
            sliding_ref[pl.ds(s * TLEN + k, LANES), :] = shifted[:, k : k + BLK]


def announce(wave_ref, flags_ref, events_ref, words_ref, held_ref):
    held_ref[...] = wave_ref[...]
    fill = jnp.zeros((2, LANES - events_ref.shape[1]), f32)
    words = jnp.concatenate([events_ref[...].astype(f32), fill], axis=1)
    words = words[0:1] + pltpu.roll(words, events_ref.shape[1], 1)[1:2]
    count = jnp.sum(flags_ref[...].astype(f32), axis=1, keepdims=True)
    lane = lax.broadcasted_iota(jnp.int32, words.shape, 1)
    words_ref[...] = jnp.broadcast_to(jnp.where(lane == SLOT - 1, count, words), words_ref.shape)


def sums_of_window(squares):
    window = jnp.broadcast_to(squares, (8, squares.shape[1]))
    width = 1
    while width < TLEN:
        window = window + left(window, width)
        width *= 2
    return window[:, :BLK]


def correlate(distances, here_ref, wave_ref, next_ref, words_ref, templates_ref, keep_ref, send_ref, sliding, own, waves, held, arrival):
    planes = len(distances)
    group = held.shape[2]
    plane, core, around = here_ref[0], here_ref[1], here_ref[3]

    def copy(i, half):
        chip = lax.rem(plane + distances[i], around) if i < planes else plane
        first = (chip * 2 + (1 - core if half == 0 else core)) * group
        target = held.at[i, half] if i < planes else own.at[half]
        return pltpu.make_async_copy(templates_ref.at[pl.ds(first, group)], target, arrival.at[i, half])

    pieces = [
        pltpu.make_async_copy(wave_ref, waves.at[0], arrival.at[planes + 1, 0]),
        pltpu.make_async_copy(next_ref, waves.at[1], arrival.at[planes + 1, 1]),
    ]
    for piece in pieces:
        piece.start()
    for i in range(planes + 1):
        for half in range(2):
            copy(i, half).start()
    for piece in pieces:
        piece.wait()
    segment = jnp.concatenate([waves[0], waves[1]], axis=1).astype(f32)
    build(segment, sliding)
    energy = sums_of_window(jnp.sum(segment * segment, axis=0, keepdims=True))
    words = jnp.concatenate([words_ref[...]] * (BLK // LANES), axis=1)
    row = lax.broadcasted_iota(jnp.int32, energy.shape, 0)
    below = jnp.where(row == WORDS, words, energy)
    keep_ref[planes * group :] = below
    send_ref[planes * group :] = below
    for i in range(planes):
        for half, out_ref in enumerate((send_ref, keep_ref)):
            copy(i, half).wait()
            filters = held[i, half].reshape(group, -1)
            out_ref[i * group : (i + 1) * group] = jnp.dot(
                filters, sliding[...], preferred_element_type=f32
            )
    for half in range(2):
        copy(planes, half).wait()


def correlate_own(own_ref, sliding_ref, keep_ref, send_ref):
    for half, out_ref in enumerate((send_ref, keep_ref)):
        filters = own_ref[half].reshape(own_ref.shape[1], -1)
        out_ref[...] = jnp.dot(filters, sliding_ref[...], preferred_element_type=f32)


def diagonal(size):
    rows = lax.broadcasted_iota(jnp.int32, (size, size), 0)
    return rows == lax.broadcasted_iota(jnp.int32, (size, size), 1)


def merge(keep_ref, came_ref, energy_ref, note_ref, *code_refs):
    half = code_refs[0].shape[0] - 8
    group = 2 * half
    square = diagonal(group)
    last = len(code_refs) * group
    energy = keep_ref[last:] + came_ref[last:]
    energy_ref[...] = energy
    words = [ref[last + WORDS : last + WORDS + 1, :LANES].astype(jnp.int32) for ref in (keep_ref, came_ref)]
    lane = lax.broadcasted_iota(jnp.int32, (1, LANES), 1)
    words = jnp.where(lane < SLOT, words[0], pltpu.roll(words[1], SLOT, 1))
    note_ref[...] = jnp.broadcast_to(words, note_ref.shape)
    logarithm = jnp.log2(jnp.maximum(energy, 1e-30))
    sample = jnp.round(4.0 * logarithm)
    level = jnp.exp2(sample[:1] * -0.125)
    power = jnp.floor(logarithm)
    bits = jnp.round(energy * jnp.exp2(23.0 - power))
    row = lax.broadcasted_iota(jnp.int32, (8, BLK), 0)
    below = jnp.where(row == 1, sample, jnp.where(row == 2, power, bits)).astype(jnp.int32)
    for i, code_ref in enumerate(code_refs):
        here = slice(i * group, (i + 1) * group)
        values = (keep_ref[here] + came_ref[here]) * level
        largest = jnp.max(jnp.abs(values), axis=1, keepdims=True)
        exponent = jnp.floor(8.0 * jnp.log2(jnp.maximum(largest, 1e-30)) + 0.01) + 1.0
        codes = jnp.round(values * (STEPS * jnp.exp2(exponent * -0.125))).astype(jnp.int32)
        code_ref[:half] = (codes[:half] & 0xFFFF) | lax.shift_left(codes[half:], 16)
        exponents = jnp.sum(jnp.where(square, exponent, 0.0), axis=0, keepdims=True)
        exponents = jnp.broadcast_to(exponents.astype(jnp.int32), (8, group))
        exponents = jnp.concatenate([exponents] * (BLK // group), axis=1)
        code_ref[half:] = jnp.where(row == 0, exponents, below)


def decode(code_ref, square):
    half = code_ref.shape[0] - 8
    words = code_ref[:half]
    codes = jnp.concatenate(
        [lax.shift_right_arithmetic(lax.shift_left(words, 16), 16), lax.shift_right_arithmetic(words, 16)],
        axis=0,
    )
    below = code_ref[half:].astype(f32)
    exponent = jnp.sum(jnp.where(square, below[:1, : 2 * half], 0.0), axis=1, keepdims=True)
    level = jnp.exp2(below[1:2] * 0.125)
    energy = below[3:4] * jnp.exp2(below[2:3] - 23.0)
    return codes.astype(f32) * (jnp.exp2(exponent * 0.125) * (1.0 / STEPS)) * level, energy


def three(values):
    high = values.astype(bf16)
    rest = values - high.astype(f32)
    middle = rest.astype(bf16)
    low = (rest - middle.astype(f32)).astype(bf16)
    return high, middle, low


def pick(selector, parts):
    return jnp.dot(jnp.concatenate([selector] * 3, axis=1), parts, preferred_element_type=f32)


def finish(keep_ref, came_ref, energy_ref, a_ref, b_ref, c_ref, flags_ref, stack_ref, parts_ref, before_ref, found_ref):
    group = stack_ref.shape[0]
    square = diagonal(group)
    stack = keep_ref[...] + came_ref[...]
    energy = energy_ref[:1]
    for code_ref in (a_ref, b_ref, c_ref):
        values, more = decode(code_ref, square)
        stack = stack + values
        energy = energy + more
    stack = stack * (1.0 / jnp.sqrt(energy + epsilon))
    stack_ref[...] = stack
    parts_ref[...] = jnp.concatenate(three(stack), axis=0)
    flags = jnp.broadcast_to(flags_ref[...], (8, group)).astype(f32)
    earlier = lax.broadcasted_iota(jnp.int32, (group, group), 0) < lax.broadcasted_iota(
        jnp.int32, (group, group), 1
    )
    before = jnp.dot(flags.astype(bf16), earlier.astype(f32).astype(bf16), preferred_element_type=f32)
    before_ref[...] = jnp.where(flags > 0.5, before, -2.0)
    found = jnp.sum(flags_ref[...], axis=1, keepdims=True)
    found_ref[...] = jnp.broadcast_to(found, found_ref.shape)


def select(here_ref, parts_ref, before_ref, found_ref, info_ref, windows_ref):
    info = info_ref[...]
    chips = info.shape[0]
    core, here = here_ref[1], here_ref[2]
    lanes = lax.broadcasted_iota(jnp.int32, info.shape, 1)
    second = lanes >= SLOT
    device = 2 * lax.broadcasted_iota(jnp.int32, info.shape, 0) + jnp.where(second, 1 - core, core)
    word = jnp.where(second, lanes - SLOT, lanes)
    start = jnp.where((word == SLOT - 1) & (device < here), info, 0)
    start = jnp.sum(jnp.sum(start, axis=0, keepdims=True), axis=1, keepdims=True)
    found = found_ref[:1, :1]
    mine = (info >= start) & (info < start + found) & (word < 32)
    rank = jnp.where(mine, info - start + 1, 0)
    ranks = [jnp.sum(jnp.where(side, rank, 0), axis=1, keepdims=True) - 1 for side in (lanes < SLOT, second)]
    ranks = [jnp.where(core == 0, ranks[k], ranks[1 - k]) for k in range(2)]
    rank = jnp.concatenate(ranks, axis=0)
    before = jnp.broadcast_to(before_ref[:1], (2 * chips, before_ref.shape[1]))
    selector = before == rank.astype(f32)
    windows = pick(selector.astype(f32).astype(bf16), parts_ref[...])
    across = BLK // LANES
    for k in range(across):
        rows = pl.ds(k, windows.shape[0], stride=across)
        windows_ref[rows, :] = windows[:, k * LANES : (k + 1) * LANES]


def choose(here_ref, events_ref, info_ref, selector_ref):
    info = info_ref[...]
    chips = info.shape[0]
    pairs = events_ref.shape[1]
    core = here_ref[1]
    counts = [jnp.where(core == k, info[:, SLOT - 1 : SLOT], info[:, LANES - 1 :]) for k in range(2)]
    rows = lax.broadcasted_iota(jnp.int32, (chips, 2 * chips), 0)
    lanes = lax.broadcasted_iota(jnp.int32, (chips, 2 * chips), 1)
    second = lanes >= chips
    chip = jnp.where(second, lanes - chips, lanes)
    earlier = jnp.where(rows < chip, counts[0] + counts[1], 0)
    earlier = earlier + jnp.where((rows == chip) & second, counts[0], 0)
    starts = jnp.sum(earlier, axis=0, keepdims=True)
    own = jnp.where(rows == chip, jnp.where(second, counts[1], counts[0]), 0)
    ends = starts + jnp.sum(own, axis=0, keepdims=True)
    square = diagonal(pairs)
    both = jnp.concatenate(
        [
            jnp.sum(jnp.where(square, events_ref[i : i + 1], 0), axis=1, keepdims=True)
            for i in range(2)
        ],
        axis=0,
    )
    selector_ref[...] = ((starts <= both) & (both < ends)).astype(f32)


def cross(lags_ref, selector_ref, received_ref, out_ref, turned, products):
    pairs = out_ref.shape[0]
    across = BLK // LANES
    sources = selector_ref.shape[1]
    received = [received_ref[pl.ds(k, sources, stride=across), :] for k in range(across)]
    picked = pick(selector_ref[...].astype(bf16), jnp.concatenate(three(jnp.concatenate(received, axis=1)), axis=0))
    first, second = picked[:pairs], picked[pairs:]
    length = 2 * BLK
    nothing = jnp.zeros((pairs, BLK), f32)
    ahead = jnp.concatenate([first, nothing], axis=1)
    behind = jnp.concatenate([second, nothing], axis=1)

    def near(values):
        return jnp.concatenate([values[:, length - NLAG :], values[:, :BLK]], axis=1)

    for u in range(NLAG // 8):
        turned[u] = near(behind if u == 0 else left(behind, 8 * u))
    for p in range(pairs):
        shift = lax.rem(lags_ref[p] + length, length)
        moved = pltpu.roll(jnp.broadcast_to(ahead[p : p + 1], (8, length)), shift, 1)
        moved = near(pltpu.roll(moved, 0, 1, stride=1, stride_axis=0))
        for u in range(NLAG // 8):
            product = moved * turned[u, pl.ds(p, 1), :]
            part = product[:, :LANES]
            for k in range(LANES, NLAG + BLK, LANES):
                part = part + product[:, k : k + LANES]
            products[pl.ds(p * NLAG + 8 * u, 8), :] = part
    ones = jnp.ones((8, LANES), bf16)
    high, middle, _ = three(products[...])
    high, middle = [
        lax.dot_general(ones, part, (((1,), (1,)), ((), ())), preferred_element_type=f32)
        for part in (high, middle)
    ]
    raw = high + middle
    raw = jnp.concatenate([raw[:1, p * NLAG : (p + 1) * NLAG] for p in range(pairs)], axis=0)
    power_one = jnp.mean(first * first, axis=1, keepdims=True)
    power_two = jnp.mean(second * second, axis=1, keepdims=True)
    out_ref[...] = raw / jnp.sqrt(BLK * (power_one + epsilon) * (power_two + epsilon))


def shards(waveforms, templates, detection_flags, pair_events, pair_lags):
    ahead, planes = lax.axis_size("tm"), lax.axis_size("z")
    chips = ahead * planes
    group = detection_flags.shape[0]
    plane, core = lax.axis_index("z"), lax.axis_index("core")
    place = (lax.axis_index("tm") * planes + plane) * 2 + core

    following = lax.ppermute(waveforms, "tm", [(i, i - 1) for i in range(1, ahead)])
    here = jnp.stack([plane, core, place, jnp.int32(planes)]).astype(jnp.int32)
    flags = detection_flags.reshape(1, group)
    events = pair_events.T
    words, waves = whole(
        announce,
        (pltpu.VMEM((8, LANES), f32), pltpu.VMEM(waveforms.shape, bf16)),
        1 << 20,
        waveforms,
        flags,
        events,
    )

    stations = templates.shape[1]
    away = (1, 3, 2)
    any_space = pl.BlockSpec(memory_space=pl.ANY)
    flops = 4 * group * stations * TLEN * BLK
    shape = pltpu.VMEM((len(away) * group + 8, BLK), f32)
    keeps, sends, sliding, own = pl.pallas_call(
        functools.partial(correlate, away),
        out_shape=(
            shape,
            shape,
            pltpu.VMEM((stations * TLEN, BLK), bf16),
            pltpu.VMEM((2, group, stations, TLEN), bf16),
        ),
        in_specs=[SMEM, any_space, any_space, VMEM, pl.BlockSpec(memory_space=pltpu.HBM)],
        out_specs=(VMEM,) * 4,
        scratch_shapes=[
            pltpu.VMEM((2, stations, BLK), bf16),
            pltpu.VMEM((len(away), 2, group, stations, TLEN), bf16),
            pltpu.SemaphoreType.DMA((len(away) + 2, 2)),
        ],
        compiler_params=pltpu.CompilerParams(vmem_limit_bytes=42 << 20),
        cost_estimate=pl.CostEstimate(
            flops=len(away) * flops, bytes_accessed=len(away) * flops // BLK, transcendentals=0
        ),
    )(here, waves, following, words, templates)

    def over(distance, values):
        return lax.ppermute(values, "z", [(i, (i + distance) % planes) for i in range(planes)])

    def swap(values):
        return lax.ppermute(values, "core", [(0, 1), (1, 0)])

    cames = swap(sends)
    shape = pltpu.VMEM((group, BLK), f32)
    keep, send = whole(correlate_own, (shape, shape), flops, own, sliding)
    came = swap(send)
    cames, _ = lax.optimization_barrier((cames, keep))
    shape = pltpu.VMEM((group // 2 + 8, BLK), jnp.int32)
    note = pltpu.VMEM((chips, LANES), jnp.int32)
    energy, note, *codes = whole(
        merge,
        (pltpu.VMEM((8, BLK), f32), note) + (shape,) * len(away),
        1 << 22,
        keeps,
        cames,
    )
    arrived = [over(distance, values) for distance, values in zip(away, codes)]
    info = lax.all_to_all(note.reshape(chips, 1, LANES), ("tm", "z"), 0, 0, tiled=True)
    info = info.reshape(chips, LANES)

    network_stack, parts, before, found = whole(
        finish,
        (
            pltpu.VMEM((group, BLK), f32),
            pltpu.VMEM((3 * group, BLK), bf16),
            pltpu.VMEM((8, group), f32),
            pltpu.VMEM((8, LANES), jnp.int32),
        ),
        1 << 24,
        keep,
        came,
        energy,
        *arrived,
        flags,
    )
    windows = whole(
        select,
        pltpu.VMEM((2 * chips * BLK // LANES, LANES), f32),
        1 << 24,
        here,
        parts,
        before,
        found,
        info,
        smem=1,
    )
    windows = windows.reshape(2 * chips, BLK // LANES, LANES)
    received = lax.all_to_all(windows, ("core", "tm", "z"), 0, 0, tiled=True)
    received = received.reshape(-1, LANES)
    pairs = pair_events.shape[0]
    selector = whole(
        choose, pltpu.VMEM((2 * pairs, 2 * chips), f32), 1 << 20, here, events, info, smem=1
    )
    pair_cc = whole(
        cross,
        jax.ShapeDtypeStruct((pairs, NLAG), f32),
        1 << 24,
        pair_lags,
        selector,
        received,
        smem=1,
        scratch=[
            pltpu.VMEM((NLAG // 8, pairs, NLAG + BLK), f32),
            pltpu.VMEM((pairs * NLAG, LANES), f32),
        ],
    )
    return (network_stack, pair_cc)


def solution(mesh):
    ahead, across = mesh.devices.shape
    split = jax.sharding.Mesh(mesh.devices.reshape(ahead, across // 2, 2), ("tm", "z", "core"))
    stations = ("z", "core")
    owners = ("tm", "z", "core")
    return jax.shard_map(
        shards,
        mesh=split,
        in_specs=(
            P(stations, "tm"),
            P(None, stations, None),
            P(stations, "tm"),
            P(owners, None),
            P(owners),
        ),
        out_specs=(P(stations, "tm"), P(owners, None)),
        check_vma=False,
    )
```

```python
import functools

import jax
import jax.numpy as jnp
from jax import lax
from jax.experimental import pallas as pl
from jax.experimental.pallas import tpu as pltpu
from jax.sharding import PartitionSpec as P

BLK = 512
TLEN = 512
NLAG = 128
LANES = 128
SLOT = 64
WORDS = 4
STEPS = 32767.0
epsilon = 1e-06
VMEM = pl.BlockSpec(memory_space=pltpu.VMEM)
SMEM = pl.BlockSpec(memory_space=pltpu.SMEM)
f32 = jnp.float32
bf16 = jnp.bfloat16


def whole(kernel, outs, flops, *operands, smem=0, scratch=()):
    return pl.pallas_call(
        kernel,
        out_shape=outs,
        in_specs=[SMEM] * smem + [VMEM] * (len(operands) - smem),
        out_specs=jax.tree.map(lambda _: VMEM, outs),
        scratch_shapes=scratch,
        compiler_params=pltpu.CompilerParams(vmem_limit_bytes=20 << 20),
        cost_estimate=pl.CostEstimate(flops=flops, bytes_accessed=1 << 20, transcendentals=0),
    )(*operands)


def left(values, distance):
    return pltpu.roll(values, values.shape[-1] - distance, values.ndim - 1)


def build(segment, sliding_ref):
    stations, length = segment.shape
    down = lax.broadcasted_iota(jnp.int32, (LANES, LANES), 0)
    along = lax.broadcasted_iota(jnp.int32, (LANES, LANES), 1)
    flip = (down + along == LANES - 1).astype(f32).astype(bf16)
    for s in range(stations):
        row = jnp.broadcast_to(segment[s : s + 1], (LANES, length))
        moved = pltpu.roll(row, length - LANES + 1, 1, stride=1, stride_axis=0).astype(bf16)
        shifted = jnp.dot(flip, moved, preferred_element_type=f32).astype(bf16)
        for k in range(0, TLEN, LANES):
            sliding_ref[pl.ds(s * TLEN + k, LANES), :] = shifted[:, k : k + BLK]


def announce(wave_ref, flags_ref, events_ref, words_ref, held_ref):
    held_ref[...] = wave_ref[...]
    fill = jnp.zeros((2, LANES - events_ref.shape[1]), f32)
    words = jnp.concatenate([events_ref[...].astype(f32), fill], axis=1)
    words = words[0:1] + pltpu.roll(words, events_ref.shape[1], 1)[1:2]
    count = jnp.sum(flags_ref[...].astype(f32), axis=1, keepdims=True)
    lane = lax.broadcasted_iota(jnp.int32, words.shape, 1)
    words_ref[...] = jnp.broadcast_to(jnp.where(lane == SLOT - 1, count, words), words_ref.shape)


def sums_of_window(squares):
    window = jnp.broadcast_to(squares, (8, squares.shape[1]))
    width = 1
    while width < TLEN:
        window = window + left(window, width)
        width *= 2
    return window[:, :BLK]


def correlate(distances, here_ref, wave_ref, next_ref, words_ref, templates_ref, keep_ref, send_ref, sliding, own, waves, held, arrival):
    planes = len(distances)
    group = held.shape[2]
    plane, core, around = here_ref[0], here_ref[1], here_ref[3]

    def copy(i, half):
        chip = lax.rem(plane + distances[i], around) if i < planes else plane
        first = (chip * 2 + (1 - core if half == 0 else core)) * group
        target = held.at[i, half] if i < planes else own.at[half]
        return pltpu.make_async_copy(templates_ref.at[pl.ds(first, group)], target, arrival.at[i, half])

    pieces = [
        pltpu.make_async_copy(wave_ref, waves.at[0], arrival.at[planes + 1, 0]),
        pltpu.make_async_copy(next_ref, waves.at[1], arrival.at[planes + 1, 1]),
    ]
    for piece in pieces:
        piece.start()
    for i in range(planes + 1):
        for half in range(2):
            copy(i, half).start()
    for piece in pieces:
        piece.wait()
    segment = jnp.concatenate([waves[0], waves[1]], axis=1).astype(f32)
    build(segment, sliding)
    energy = sums_of_window(jnp.sum(segment * segment, axis=0, keepdims=True))
    words = jnp.concatenate([words_ref[...]] * (BLK // LANES), axis=1)
    row = lax.broadcasted_iota(jnp.int32, energy.shape, 0)
    below = jnp.where(row == WORDS, words, energy)
    keep_ref[planes * group :] = below
    send_ref[planes * group :] = below
    for i in range(planes):
        for half, out_ref in enumerate((send_ref, keep_ref)):
            copy(i, half).wait()
            filters = held[i, half].reshape(group, -1)
            out_ref[i * group : (i + 1) * group] = jnp.dot(
                filters, sliding[...], preferred_element_type=f32
            )
    for half in range(2):
        copy(planes, half).wait()


def correlate_own(own_ref, sliding_ref, keep_ref, send_ref):
    for half, out_ref in enumerate((send_ref, keep_ref)):
        filters = own_ref[half].reshape(own_ref.shape[1], -1)
        out_ref[...] = jnp.dot(filters, sliding_ref[...], preferred_element_type=f32)


def diagonal(size):
    rows = lax.broadcasted_iota(jnp.int32, (size, size), 0)
    return rows == lax.broadcasted_iota(jnp.int32, (size, size), 1)


def merge(keep_ref, came_ref, energy_ref, note_ref, *code_refs):
    half = code_refs[0].shape[0] - 8
    group = 2 * half
    square = diagonal(group)
    last = len(code_refs) * group
    energy = keep_ref[last:] + came_ref[last:]
    energy_ref[...] = energy
    words = [ref[last + WORDS : last + WORDS + 1, :LANES].astype(jnp.int32) for ref in (keep_ref, came_ref)]
    lane = lax.broadcasted_iota(jnp.int32, (1, LANES), 1)
    words = jnp.where(lane < SLOT, words[0], pltpu.roll(words[1], SLOT, 1))
    note_ref[...] = jnp.broadcast_to(words, note_ref.shape)
    logarithm = jnp.log2(jnp.maximum(energy, 1e-30))
    sample = jnp.round(4.0 * logarithm)
    level = jnp.exp2(sample[:1] * -0.125)
    power = jnp.floor(logarithm)
    bits = jnp.round(energy * jnp.exp2(23.0 - power))
    row = lax.broadcasted_iota(jnp.int32, (8, BLK), 0)
    below = jnp.where(row == 1, sample, jnp.where(row == 2, power, bits)).astype(jnp.int32)
    for i, code_ref in enumerate(code_refs):
        here = slice(i * group, (i + 1) * group)
        values = (keep_ref[here] + came_ref[here]) * level
        largest = jnp.max(jnp.abs(values), axis=1, keepdims=True)
        exponent = jnp.floor(8.0 * jnp.log2(jnp.maximum(largest, 1e-30)) + 0.01) + 1.0
        codes = jnp.round(values * (STEPS * jnp.exp2(exponent * -0.125))).astype(jnp.int32)
        code_ref[:half] = (codes[:half] & 0xFFFF) | lax.shift_left(codes[half:], 16)
        exponents = jnp.sum(jnp.where(square, exponent, 0.0), axis=0, keepdims=True)
        exponents = jnp.broadcast_to(exponents.astype(jnp.int32), (8, group))
        exponents = jnp.concatenate([exponents] * (BLK // group), axis=1)
        code_ref[half:] = jnp.where(row == 0, exponents, below)


def decode(code_ref, square):
    half = code_ref.shape[0] - 8
    words = code_ref[:half]
    codes = jnp.concatenate(
        [lax.shift_right_arithmetic(lax.shift_left(words, 16), 16), lax.shift_right_arithmetic(words, 16)],
        axis=0,
    )
    below = code_ref[half:].astype(f32)
    exponent = jnp.sum(jnp.where(square, below[:1, : 2 * half], 0.0), axis=1, keepdims=True)
    level = jnp.exp2(below[1:2] * 0.125)
    energy = below[3:4] * jnp.exp2(below[2:3] - 23.0)
    return codes.astype(f32) * (jnp.exp2(exponent * 0.125) * (1.0 / STEPS)) * level, energy


def halves(values):
    high = values.astype(bf16)
    return high, (values - high.astype(f32)).astype(bf16)


def pick(selector, parts):
    return jnp.dot(jnp.concatenate([selector] * 2, axis=1), parts, preferred_element_type=f32)


def finish(keep_ref, came_ref, energy_ref, a_ref, b_ref, c_ref, flags_ref, stack_ref, parts_ref, before_ref, found_ref):
    group = stack_ref.shape[0]
    square = diagonal(group)
    stack = keep_ref[...] + came_ref[...]
    energy = energy_ref[:1]
    for code_ref in (a_ref, b_ref, c_ref):
        values, more = decode(code_ref, square)
        stack = stack + values
        energy = energy + more
    stack = stack * (1.0 / jnp.sqrt(energy + epsilon))
    stack_ref[...] = stack
    parts_ref[...] = jnp.concatenate(halves(stack), axis=0)
    flags = jnp.broadcast_to(flags_ref[...], (8, group)).astype(f32)
    earlier = lax.broadcasted_iota(jnp.int32, (group, group), 0) < lax.broadcasted_iota(
        jnp.int32, (group, group), 1
    )
    before = jnp.dot(flags.astype(bf16), earlier.astype(f32).astype(bf16), preferred_element_type=f32)
    before_ref[...] = jnp.where(flags > 0.5, before, -2.0)
    found = jnp.sum(flags_ref[...], axis=1, keepdims=True)
    found_ref[...] = jnp.broadcast_to(found, found_ref.shape)


def select(here_ref, parts_ref, before_ref, found_ref, info_ref, windows_ref):
    info = info_ref[...]
    chips = info.shape[0]
    core, here = here_ref[1], here_ref[2]
    lanes = lax.broadcasted_iota(jnp.int32, info.shape, 1)
    second = lanes >= SLOT
    device = 2 * lax.broadcasted_iota(jnp.int32, info.shape, 0) + jnp.where(second, 1 - core, core)
    word = jnp.where(second, lanes - SLOT, lanes)
    start = jnp.where((word == SLOT - 1) & (device < here), info, 0)
    start = jnp.sum(jnp.sum(start, axis=0, keepdims=True), axis=1, keepdims=True)
    found = found_ref[:1, :1]
    mine = (info >= start) & (info < start + found) & (word < 32)
    rank = jnp.where(mine, info - start + 1, 0)
    ranks = [jnp.sum(jnp.where(side, rank, 0), axis=1, keepdims=True) - 1 for side in (lanes < SLOT, second)]
    ranks = [jnp.where(core == 0, ranks[k], ranks[1 - k]) for k in range(2)]
    rank = jnp.concatenate(ranks, axis=0)
    before = jnp.broadcast_to(before_ref[:1], (2 * chips, before_ref.shape[1]))
    selector = before == rank.astype(f32)
    windows = pick(selector.astype(f32).astype(bf16), parts_ref[...])
    across = BLK // LANES
    for k in range(across):
        rows = pl.ds(k, windows.shape[0], stride=across)
        windows_ref[rows, :] = windows[:, k * LANES : (k + 1) * LANES]


def choose(here_ref, events_ref, info_ref, selector_ref):
    info = info_ref[...]
    chips = info.shape[0]
    pairs = events_ref.shape[1]
    core = here_ref[1]
    counts = [jnp.where(core == k, info[:, SLOT - 1 : SLOT], info[:, LANES - 1 :]) for k in range(2)]
    rows = lax.broadcasted_iota(jnp.int32, (chips, 2 * chips), 0)
    lanes = lax.broadcasted_iota(jnp.int32, (chips, 2 * chips), 1)
    second = lanes >= chips
    chip = jnp.where(second, lanes - chips, lanes)
    earlier = jnp.where(rows < chip, counts[0] + counts[1], 0)
    earlier = earlier + jnp.where((rows == chip) & second, counts[0], 0)
    starts = jnp.sum(earlier, axis=0, keepdims=True)
    own = jnp.where(rows == chip, jnp.where(second, counts[1], counts[0]), 0)
    ends = starts + jnp.sum(own, axis=0, keepdims=True)
    square = diagonal(pairs)
    both = jnp.concatenate(
        [
            jnp.sum(jnp.where(square, events_ref[i : i + 1], 0), axis=1, keepdims=True)
            for i in range(2)
        ],
        axis=0,
    )
    selector_ref[...] = ((starts <= both) & (both < ends)).astype(f32)


def cross(lags_ref, selector_ref, received_ref, out_ref, turned, products):
    pairs = out_ref.shape[0]
    across = BLK // LANES
    sources = selector_ref.shape[1]
    received = [received_ref[pl.ds(k, sources, stride=across), :] for k in range(across)]
    picked = pick(selector_ref[...].astype(bf16), jnp.concatenate(halves(jnp.concatenate(received, axis=1)), axis=0))
    first, second = picked[:pairs], picked[pairs:]
    length = 2 * BLK
    nothing = jnp.zeros((pairs, BLK), f32)
    ahead = jnp.concatenate([first, nothing], axis=1)
    behind = jnp.concatenate([second, nothing], axis=1)

    def near(values):
        return jnp.concatenate([values[:, length - NLAG :], values[:, :BLK]], axis=1)

    for u in range(NLAG // 8):
        turned[u] = near(behind if u == 0 else left(behind, 8 * u))
    for p in range(pairs):
        shift = lax.rem(lags_ref[p] + length, length)
        moved = pltpu.roll(jnp.broadcast_to(ahead[p : p + 1], (8, length)), shift, 1)
        moved = near(pltpu.roll(moved, 0, 1, stride=1, stride_axis=0))
        for u in range(NLAG // 8):
            product = moved * turned[u, pl.ds(p, 1), :]
            part = product[:, :LANES]
            for k in range(LANES, NLAG + BLK, LANES):
                part = part + product[:, k : k + LANES]
            products[pl.ds(p * NLAG + 8 * u, 8), :] = part
    ones = jnp.ones((8, LANES), bf16)
    high, middle = [
        lax.dot_general(ones, part, (((1,), (1,)), ((), ())), preferred_element_type=f32)
        for part in halves(products[...])
    ]
    raw = high + middle
    raw = jnp.concatenate([raw[:1, p * NLAG : (p + 1) * NLAG] for p in range(pairs)], axis=0)
    power_one = jnp.mean(first * first, axis=1, keepdims=True)
    power_two = jnp.mean(second * second, axis=1, keepdims=True)
    out_ref[...] = raw / jnp.sqrt(BLK * (power_one + epsilon) * (power_two + epsilon))


def shards(waveforms, templates, detection_flags, pair_events, pair_lags):
    ahead, planes = lax.axis_size("tm"), lax.axis_size("z")
    chips = ahead * planes
    group = detection_flags.shape[0]
    plane, core = lax.axis_index("z"), lax.axis_index("core")
    place = (lax.axis_index("tm") * planes + plane) * 2 + core

    following = lax.ppermute(waveforms, "tm", [(i, i - 1) for i in range(1, ahead)])
    here = jnp.stack([plane, core, place, jnp.int32(planes)]).astype(jnp.int32)
    flags = detection_flags.reshape(1, group)
    events = pair_events.T
    words, waves = whole(
        announce,
        (pltpu.VMEM((8, LANES), f32), pltpu.VMEM(waveforms.shape, bf16)),
        1 << 20,
        waveforms,
        flags,
        events,
    )

    stations = templates.shape[1]
    away = (2, 1, 3)
    any_space = pl.BlockSpec(memory_space=pl.ANY)
    flops = 4 * group * stations * TLEN * BLK
    shape = pltpu.VMEM((len(away) * group + 8, BLK), f32)
    keeps, sends, sliding, own = pl.pallas_call(
        functools.partial(correlate, away),
        out_shape=(
            shape,
            shape,
            pltpu.VMEM((stations * TLEN, BLK), bf16),
            pltpu.VMEM((2, group, stations, TLEN), bf16),
        ),
        in_specs=[SMEM, any_space, any_space, VMEM, pl.BlockSpec(memory_space=pltpu.HBM)],
        out_specs=(VMEM,) * 4,
        scratch_shapes=[
            pltpu.VMEM((2, stations, BLK), bf16),
            pltpu.VMEM((len(away), 2, group, stations, TLEN), bf16),
            pltpu.SemaphoreType.DMA((len(away) + 2, 2)),
        ],
        compiler_params=pltpu.CompilerParams(vmem_limit_bytes=42 << 20),
        cost_estimate=pl.CostEstimate(
            flops=len(away) * flops, bytes_accessed=len(away) * flops // BLK, transcendentals=0
        ),
    )(here, waves, following, words, templates)

    def over(distance, values):
        return lax.ppermute(values, "z", [(i, (i + distance) % planes) for i in range(planes)])

    def swap(values):
        return lax.ppermute(values, "core", [(0, 1), (1, 0)])

    cames = swap(sends)
    shape = pltpu.VMEM((group, BLK), f32)
    keep, send = whole(correlate_own, (shape, shape), flops, own, sliding)
    came = swap(send)
    cames, _ = lax.optimization_barrier((cames, keep))
    shape = pltpu.VMEM((group // 2 + 8, BLK), jnp.int32)
    note = pltpu.VMEM((chips, LANES), jnp.int32)
    energy, note, *codes = whole(
        merge,
        (pltpu.VMEM((8, BLK), f32), note) + (shape,) * len(away),
        1 << 22,
        keeps,
        cames,
    )
    arrived = [over(distance, values) for distance, values in zip(away, codes)]
    info = lax.all_to_all(note.reshape(chips, 1, LANES), ("tm", "z"), 0, 0, tiled=True)
    info = info.reshape(chips, LANES)

    network_stack, parts, before, found = whole(
        finish,
        (
            pltpu.VMEM((group, BLK), f32),
            pltpu.VMEM((2 * group, BLK), bf16),
            pltpu.VMEM((8, group), f32),
            pltpu.VMEM((8, LANES), jnp.int32),
        ),
        1 << 24,
        keep,
        came,
        energy,
        *arrived,
        flags,
    )
    windows = whole(
        select,
        pltpu.VMEM((2 * chips * BLK // LANES, LANES), f32),
        1 << 24,
        here,
        parts,
        before,
        found,
        info,
        smem=1,
    )
    windows = windows.reshape(2 * chips, BLK // LANES, LANES)
    received = lax.all_to_all(windows, ("core", "tm", "z"), 0, 0, tiled=True)
    received = received.reshape(-1, LANES)
    pairs = pair_events.shape[0]
    selector = whole(
        choose, pltpu.VMEM((2 * pairs, 2 * chips), f32), 1 << 20, here, events, info, smem=1
    )
    pair_cc = whole(
        cross,
        jax.ShapeDtypeStruct((pairs, NLAG), f32),
        1 << 24,
        pair_lags,
        selector,
        received,
        smem=1,
        scratch=[
            pltpu.VMEM((NLAG // 8, pairs, NLAG + BLK), f32),
            pltpu.VMEM((pairs * NLAG, LANES), f32),
        ],
    )
    return (network_stack, pair_cc)


def solution(mesh):
    ahead, across = mesh.devices.shape
    split = jax.sharding.Mesh(mesh.devices.reshape(ahead, across // 2, 2), ("tm", "z", "core"))
    stations = ("z", "core")
    owners = ("tm", "z", "core")
    return jax.shard_map(
        shards,
        mesh=split,
        in_specs=(
            P(stations, "tm"),
            P(None, stations, None),
            P(stations, "tm"),
            P(owners, None),
            P(owners),
        ),
        out_specs=(P(stations, "tm"), P(owners, None)),
        check_vma=False,
    )
```
